512 devices in a mesh: node: 128 (over y, z, core), head: 4 (over x).
Axes of the slice: x: 4, y: 4, z: 16, core: 2. Of those that a mesh axis runs over, the one named last changes fastest.
Arguments:
- queries: bfloat16 [4096, 8192], P(('node', 'head')), may hold values from -128 to 128
- kv_cache: bfloat16 [2, 128, 512, 512], P(None, 'node', None, 'head'), may hold values from -6 to 6
- node_len: int32 [128], P('node'), may hold values from 128 to 512
- paths: int32 [4096, 4], P('node'), may hold values from 0 to 127, as said below
Outputs:
- attended: bfloat16 [4096, 8192], P(('node', 'head'))
The draws below stay inside these ranges and needn't reach their ends.
Inputs may be any that keep to these rules, and one draw needn't show every extreme that they name: The rows' paths follow one tree of 128 nodes: 16 first-level nodes with one child each, each such child with two children, each of these with two leaf children; a row's entries are a first-level node and its descendants down to a leaf. In every aligned block of 32 rows (the rows of one index of node) each first-level node and its child lie on the paths of exactly 2 rows, and no node lies on more than 2 rows of the block.
All inputs are finite; a program needn't handle non-finite values.
Results may differ from the reference program's by a relative error of at most 0.0056.
Values may be sent and summed in bfloat16 or wider, within the bound.
A program may use at most 64 MiB of HBM per device.

```python
import jax
import jax.numpy as jnp
from jax import lax

QHEADS = 64
KV_HEADS = 4
HEAD_DIM = 128
NODE_LEN = 512
DEPTH = 4
GROUP = 16
NODES = 128
ROWS_NODE = 32
ROWS = 4096
CAP = 2


def tree_paths(key):
    base_key = jax.random.fold_in(key, 101)
    key_order, key_rows, key_bits = jax.random.split(base_key, 3)
    root_count = NODES // 8
    node_order = jax.random.permutation(key_order, NODES).astype(jnp.int32)
    group_keys = jax.random.split(key_rows, ROWS // ROWS_NODE)
    row_orders = jax.vmap(lambda group_key: jax.random.permutation(group_key, ROWS_NODE))(group_keys)
    root_index = (row_orders.reshape(-1) // CAP).astype(jnp.int32)
    branch_bits = jax.random.randint(key_bits, (ROWS, 2), 0, 2, dtype=jnp.int32)
    middle = 2 * root_index + branch_bits[:, 0]
    leaf_index = 2 * middle + branch_bits[:, 1]
    level_index = jnp.stack([root_index, root_count + root_index, 2 * root_count + middle, 4 * root_count + leaf_index], axis=1)
    return node_order[level_index]


def first_keys(key):
    return jax.random.truncated_normal(jax.random.fold_in(key, 7), -6.0, 6.0, (NODES, KV_HEADS * HEAD_DIM), jnp.float32)


def draw_paths(key, part):
    return tree_paths(key)


def draw_kv_cache(key, part):
    leading = first_keys(key)
    key = jax.random.fold_in(key, 3)
    table = jax.random.truncated_normal(key, -6.0, 6.0, (2, NODES, NODE_LEN, KV_HEADS * HEAD_DIM), jnp.float32)
    table = table.at[0, :, 0, :].set(leading)
    return table.astype(jnp.bfloat16)


def draw_queries(key, part):
    key = jax.random.fold_in(key, 5)
    values = jax.random.truncated_normal(key, -6.0, 6.0, (ROWS, QHEADS * HEAD_DIM), jnp.float32)
    return values.astype(jnp.bfloat16)


def draw_node_len(key, part):
    key = jax.random.fold_in(key, 9)
    counts = jax.random.randint(key, (NODES,), NODE_LEN // 4, NODE_LEN + 1, dtype=jnp.int32)
    chosen = jax.random.randint(jax.random.fold_in(key, 1), (), 0, NODES, dtype=jnp.int32)
    return counts.at[chosen].set(NODE_LEN)


def setup_inputs(seed: int = 0) -> dict:
    keys = jax.random.split(jax.random.key(seed), 5)
    queries = draw_queries(jax.random.fold_in(keys[4], 71), 0)
    kv_cache = draw_kv_cache(jax.random.fold_in(keys[4], 71), 0)
    node_len = draw_node_len(jax.random.fold_in(keys[4], 71), 0)
    paths = draw_paths(jax.random.fold_in(keys[4], 71), 0)
    return {"queries": queries, "kv_cache": kv_cache, "node_len": node_len, "paths": paths}


def merge_parts(outs, peaks, totals):
    top_peak = jnp.max(peaks, axis=1, keepdims=True)
    weight = jnp.exp(peaks - top_peak)
    numerator = jnp.sum(weight[..., None] * outs.astype(jnp.float32), axis=1)
    denominator = jnp.sum(weight * totals, axis=1)
    return numerator / denominator[..., None]


def reference(queries, kv_cache, node_len, paths):
    score_scale = HEAD_DIM ** -0.5
    key_table = kv_cache[0].reshape(NODES, NODE_LEN, KV_HEADS, HEAD_DIM)
    value_table = kv_cache[1].reshape(NODES, NODE_LEN, KV_HEADS, HEAD_DIM)
    positions = jnp.arange(NODE_LEN, dtype=jnp.int32)
    query_blocks = queries.reshape(ROWS // ROWS_NODE, ROWS_NODE, KV_HEADS, GROUP, HEAD_DIM)
    path_blocks = paths.reshape(ROWS // ROWS_NODE, ROWS_NODE, DEPTH)

    def attend_rows(pair):
        query_block, path_block = pair
        query_full = query_block.astype(jnp.float32)
        key_full = key_table[path_block].astype(jnp.float32)
        value_full = value_table[path_block].astype(jnp.float32)
        scores = jnp.einsum("bhgd,bnlhd->bnhgl", query_full, key_full, precision=lax.Precision.HIGHEST) * score_scale
        in_range = positions[None, None, :] < node_len[path_block][:, :, None]
        scores = jnp.where(in_range[:, :, None, None, :], scores, -jnp.inf)
        peak_score = jnp.max(scores, axis=-1)
        probabilities = jnp.exp(scores - peak_score[..., None])
        total_sum = jnp.sum(probabilities, axis=-1)
        rounded = lax.optimization_barrier(probabilities.astype(jnp.bfloat16)).astype(jnp.float32)
        partial_value = jnp.einsum("bnhgl,bnlhd->bnhgd", rounded, value_full, precision=lax.Precision.HIGHEST)
        partial_value = lax.optimization_barrier(partial_value.astype(jnp.bfloat16))
        merged = merge_parts(partial_value.reshape(ROWS_NODE, DEPTH, QHEADS, HEAD_DIM),
                             peak_score.reshape(ROWS_NODE, DEPTH, QHEADS),
                             total_sum.reshape(ROWS_NODE, DEPTH, QHEADS))
        return merged.reshape(ROWS_NODE, QHEADS * HEAD_DIM).astype(jnp.bfloat16)

    result = lax.map(attend_rows, (query_blocks, path_blocks))
    return result.reshape(ROWS, QHEADS * HEAD_DIM)
```

```python
import functools
import math

import jax
import jax.numpy as jnp
from jax import lax
from jax.experimental import pallas as pl
from jax.experimental.pallas import tpu as pltpu
from jax.sharding import PartitionSpec as P

MESH = pl.DeviceIdType.MESH
NX, NY, NZ, NC = 4, 4, 16, 2
PLANE = NY * NC
FAR = NZ // 2
ROWS, GROUP, DIM, TOKENS, DEPTH = 32, 16, 128, 512, 4
PAIRS = ROWS // 2
HALF = ROWS // 2
OWN = ROWS // NX
EMPTY = -1e30
SCALE = math.log2(math.e) / math.sqrt(DIM)
FLOWS = ((0, 0), (1, 1), (0, 1), (1, 0))


def reach(side, half):
    return FAR if side == half else FAR - 1


def slot(side, hop):
    return hop % NZ if side == 0 else (NZ - hop) % NZ


def kernel(
    q_ref, kv_ref, meta_ref, meta_s, len_s, out_ref,
    qx, q0, qall, kvall, lens, bias, metav, metas, part_o, part_m, part_l,
    loc_o, loc_s, o_in, o_out, s_in, s_out, fin, fx,
    x_send, x_recv, kv_send, kv_recv, ln_send, ln_recv, q_send, q_recv, m_send, m_recv,
    ms_sem, o_send, o_recv, st_send, st_recv, r_send, r_recv, own_sem,
):
    node = lax.axis_index("node")
    x = lax.axis_index("head")
    core = lax.rem(node, NC)
    z = lax.rem(node // NC, NZ)
    y = node // (NC * NZ)

    def dev(yy, zz, cc, xx):
        return ((yy * NZ + zz) * NC + cc, xx)

    z_up, z_down = lax.rem(z + 1, NZ), lax.rem(z + NZ - 1, NZ)
    out_dev = (dev(y, z_up, core, x), dev(y, z_down, core, x))
    back_dev = (out_dev[1], out_dev[0])
    mate = dev(y, z, 1 - core, x)
    y_dev = [None] + [dev(lax.rem(y + d, NY), z, core, x) for d in range(1, NY)]
    x_dev = [None] + [dev(y, z, core, lax.rem(x + d, NX)) for d in range(1, NX)]

    barrier = pltpu.get_barrier_semaphore()
    partners = [out_dev[0], out_dev[1], mate] + y_dev[1:] + x_dev[1:]
    for partner in partners:
        pl.semaphore_signal(barrier, inc=1, device_id=partner, device_id_type=MESH)
    pl.semaphore_wait(barrier, len(partners))

    def remote(src, dst, send, recv, to):
        return pltpu.make_async_remote_copy(
            src_ref=src, dst_ref=dst, send_sem=send, recv_sem=recv, device_id=to, device_id_type=MESH)

    def x_copy(d):
        heads = pl.ds(pl.multiple_of(lax.rem(x + d, NX) * GROUP, GROUP), GROUP)
        rows = pl.ds(pl.multiple_of(x * OWN, OWN), OWN)
        if d == 0:
            return pltpu.make_async_copy(q_ref.at[:, heads, :], qx.at[rows], own_sem.at[0])
        return remote(q_ref.at[:, heads, :], qx.at[rows], x_send.at[d], x_recv.at[d], x_dev[d])

    for d in (1, 2, 3, 0):
        x_copy(d).start()

    def node_of(yy, cc):
        return yy * NC + cc

    own_k = node_of(y, core)
    lens[own_k] = jnp.full(lens.shape[1:], len_s[0], jnp.int32)
    kv_own = pltpu.make_async_copy(kv_ref.at[:, 0], kvall.at[own_k], own_sem.at[1])
    kv_own.start()

    def kv_copies(kind, d):
        if kind == 0:
            k = own_k
            to = mate if d == 0 else y_dev[d]
            src = kv_ref.at[:, 0]
        else:
            k = node_of(lax.rem(y + NY - d, NY), core)
            to = mate
            src = kvall.at[k]
        i = d if kind == 0 else NY + d
        return (
            remote(src, kvall.at[k], kv_send.at[i], kv_recv.at[i], to),
            remote(lens.at[k], lens.at[k], ln_send.at[i], ln_recv.at[i], to),
        )

    for d in (2, 1, 3, 0):
        for copy in kv_copies(0, d):
            copy.start()

    for d in (0, 1, 2, 3):
        if d == 0:
            x_copy(d).wait()
        else:
            x_copy(d).wait_recv()
    for p in range(ROWS):
        q0[p // 2, (p % 2) * GROUP:(p % 2 + 1) * GROUP, :] = qx[meta_s[2, p]]

    def q_copy(side, half, hop):
        part = pl.ds(half * (PAIRS // 2), PAIRS // 2)
        src = q0.at[part] if hop == 1 else qall.at[slot(side, hop - 1), part]
        return remote(src, qall.at[slot(side, hop), part], q_send.at[side, half, hop - 1],
                      q_recv.at[side, half, hop - 1], out_dev[side])

    def m_copy(side, hop):
        src = meta_ref if hop == 1 else metav.at[slot(side, hop - 1)]
        return remote(src, metav.at[slot(side, hop)], m_send.at[side, hop - 1],
                      m_recv.at[side, hop - 1], out_dev[side])

    def m_local(i):
        src = meta_ref if i == 0 else metav.at[i]
        return pltpu.make_async_copy(src, metas.at[i], ms_sem.at[i])

    for side, half in FLOWS:
        q_copy(side, half, 1).start()
    for side in (0, 1):
        m_copy(side, 1).start()
    m_local(0).start()

    part_o[...] = jnp.zeros_like(part_o)
    part_l[...] = jnp.zeros_like(part_l)
    part_m[...] = jnp.full_like(part_m, EMPTY)

    lane = lax.broadcasted_iota(jnp.int32, (GROUP, DIM), 1)

    def attend(blocks):
        for k in range(PLANE):
            n = ((k // NC) * NZ + z) * NC + k % NC
            tiles = [ref[metas[i, 0, n]] for ref, i in blocks]
            lhs = tiles[0] if len(tiles) == 1 else jnp.concatenate(tiles, axis=0)
            score = lax.dot_general(lhs, kvall[k, 0], (((1,), (1,)), ((), ())),
                                    preferred_element_type=jnp.float32)
            score = score + bias[k:k + 1, :]
            peak = jnp.max(score, axis=1, keepdims=True)
            prob = jnp.exp2((score - peak) * SCALE)
            total = jnp.sum(prob, axis=1, keepdims=True)
            value = jnp.dot(prob.astype(jnp.bfloat16), kvall[k, 1], preferred_element_type=jnp.float32)
            for b in range(len(blocks)):
                rows = slice(b * 2 * GROUP, (b + 1) * 2 * GROUP)
                part_o[b, k] = value[rows]
                part_m[b, k] = jnp.broadcast_to(peak[rows], (2 * GROUP, DIM))
                part_l[b, k] = jnp.broadcast_to(total[rows], (2 * GROUP, DIM))

    def merge_rows(b, i, half, keep):
        stat = jnp.zeros((GROUP, DIM), jnp.float32)
        for r in range(HALF):
            p = half * HALF + r
            sub = slice((p % 2) * GROUP, (p % 2 + 1) * GROUP)
            ks = []
            for j in range(DEPTH):
                t = metas[i, 1, p * DEPTH + j] - z * NZ
                ks.append(jnp.where((t >= 0) & (t < PLANE), t, PLANE))
            peaks = [part_m[b, k, sub, :] for k in ks]
            top = jnp.maximum(jnp.maximum(peaks[0], peaks[1]), jnp.maximum(peaks[2], peaks[3]))
            total = jnp.zeros((GROUP, DIM), jnp.float32)
            value = jnp.zeros((GROUP, DIM), jnp.float32)
            for k, peak in zip(ks, peaks):
                weight = jnp.exp2((peak - top) * SCALE)
                total = total + weight * part_l[b, k, sub, :]
                value = value + weight * part_o[b, k, sub, :]
            loc_o[keep, p] = value
            stat = jnp.where(lane == r, top, jnp.where(lane == r + HALF, total, stat))
        loc_s[keep, half] = stat

    def weights(a, c):
        top = jnp.maximum(a, c)
        wa, wc = jnp.exp2((a - top) * SCALE), jnp.exp2((c - top) * SCALE)
        total = pltpu.roll(wa, HALF, 1) * a + pltpu.roll(wc, HALF, 1) * c
        return wa, wc, jnp.where(lane < HALF, top, total)

    def column(tile, r):
        return jnp.broadcast_to(tile[:, r:r + 1], (GROUP, DIM))

    def o_copies(side, half, d):
        return (
            remote(o_out.at[side, half, d - 1], o_in.at[side, half, d - 1], o_send.at[side, half, d - 1],
                   o_recv.at[side, half, d - 1], back_dev[side]),
            remote(s_out.at[side, half, d - 1], s_in.at[side, half, d - 1], st_send.at[side, half, d - 1],
                   st_recv.at[side, half, d - 1], back_dev[side]),
        )

    def first_out(side, half, d, keep):
        for r in range(HALF):
            o_out[side, half, d - 1, r] = loc_o[keep, half * HALF + r].astype(jnp.bfloat16)
        s_out[side, half, d - 1] = loc_s[keep, half]
        for copy in o_copies(side, half, d):
            copy.start()

    def add_out(side, half, d, keep):
        for copy in o_copies(side, half, d + 1):
            copy.wait_recv()
        wa, wc, stat = weights(s_in[side, half, d], loc_s[keep, half])
        s_out[side, half, d - 1] = stat
        for r in range(HALF):
            total = (column(wa, r) * o_in[side, half, d, r].astype(jnp.float32)
                     + column(wc, r) * loc_o[keep, half * HALF + r])
            o_out[side, half, d - 1, r] = total.astype(jnp.bfloat16)
        for copy in o_copies(side, half, d):
            copy.start()

    for hop in range(1, FAR + 1):
        for side, half in FLOWS:
            if hop <= reach(side, half):
                q_copy(side, half, hop).wait_recv()
                if hop < reach(side, half):
                    q_copy(side, half, hop + 1).start()
        for side in (0, 1):
            if hop <= reach(side, 0):
                m_copy(side, hop).wait_recv()
                if hop < reach(side, 0):
                    m_copy(side, hop + 1).start()
                m_local(slot(side, hop)).start()
        if hop == 5:
            for d in (1, 3, 2):
                for copy, onward in zip(kv_copies(0, d), kv_copies(1, d)):
                    copy.wait_recv()
                    onward.start()
    kv_own.wait()
    for copy in kv_copies(0, 0):
        copy.wait_recv()
    for d in (1, 3, 2):
        for copy in kv_copies(1, d):
            copy.wait_recv()
    token = lax.broadcasted_iota(jnp.int32, (1, TOKENS), 1)
    for k in range(PLANE):
        length = jnp.concatenate([lens[k, 0:1, :]] * (TOKENS // DIM), axis=1)
        bias[k:k + 1, :] = jnp.where(token < length, 0.0, EMPTY)
    for i in range(NZ):
        m_local(i).wait()

    attend([(qall.at[FAR], FAR)])
    for half in (0, 1):
        merge_rows(0, FAR, half, 0)
        first_out(half, half, FAR, 0)

    def near(d, first):
        attend([(qall.at[d], d), (qall.at[NZ - d], NZ - d)])
        for side, half in FLOWS:
            merge_rows(side, (d, NZ - d)[side], half, side)
            if first and side != half:
                first_out(side, half, d, side)
            else:
                add_out(side, half, d, side)

    near(FAR - 1, True)

    def step(t, carry):
        near(FAR - 2 - t, False)
        return carry

    lax.fori_loop(0, FAR - 2, step, 0)

    attend([(q0, 0)])
    for half in (0, 1):
        merge_rows(0, 0, half, 0)
        for side in (0, 1):
            for copy in o_copies(side, half, 1):
                copy.wait_recv()
        a, c, own = s_in[0, half, 0], s_in[1, half, 0], loc_s[0, half]
        top = jnp.maximum(jnp.maximum(a, c), own)
        wa, wc, wo = (jnp.exp2((v - top) * SCALE) for v in (a, c, own))
        total = (pltpu.roll(wa, HALF, 1) * a + pltpu.roll(wc, HALF, 1) * c + pltpu.roll(wo, HALF, 1) * own)
        share = 1.0 / jnp.where(lane >= HALF, jnp.where(lane < 2 * HALF, total, 1.0), 1.0)
        share = pltpu.roll(share, DIM - HALF, 1)
        wa, wc, wo = wa * share, wc * share, wo * share
        for r in range(HALF):
            p = half * HALF + r
            value = (column(wa, r) * o_in[0, half, 0, r].astype(jnp.float32)
                     + column(wc, r) * o_in[1, half, 0, r].astype(jnp.float32)
                     + column(wo, r) * loc_o[0, p])
            fin[p] = value.astype(jnp.bfloat16)

    for r in range(ROWS):
        fx[r] = fin[meta_s[2, ROWS + r]]

    def r_copy(d):
        rows = pl.ds(pl.multiple_of(lax.rem(x + d, NX) * OWN, OWN), OWN)
        heads = pl.ds(pl.multiple_of(x * GROUP, GROUP), GROUP)
        if d == 0:
            return pltpu.make_async_copy(fx.at[rows], out_ref.at[:, heads, :], own_sem.at[2])
        return remote(fx.at[rows], out_ref.at[:, heads, :], r_send.at[d], r_recv.at[d], x_dev[d])

    for d in (1, 2, 3, 0):
        r_copy(d).start()
    for d in (1, 2, 3):
        x_copy(d).wait_send()
    for d in range(NY):
        for kind in (0, 1):
            if kind == 0 or d > 0:
                for copy in kv_copies(kind, d):
                    copy.wait_send()
    for hop in range(1, FAR + 1):
        for side, half in FLOWS:
            if hop <= reach(side, half):
                q_copy(side, half, hop).wait_send()
                for copy in o_copies(side, half, hop):
                    copy.wait_send()
        for side in (0, 1):
            if hop <= reach(side, 0):
                m_copy(side, hop).wait_send()
    r_copy(0).wait()
    for d in (1, 2, 3):
        r_copy(d).wait()


def plan(paths):
    row = jnp.arange(ROWS, dtype=jnp.int32)
    key = paths[:, 0] * ROWS + row
    place = jnp.sum((key[None, :] < key[:, None]).astype(jnp.int32), axis=1)
    at = (place[None, :] == row[:, None]).astype(jnp.int32)
    order = jnp.sum(at * row[None, :], axis=1)
    ordered = jnp.sum(at[:, :, None] * paths[None, :, :], axis=1)
    nodes = jnp.arange(PLANE * NZ, dtype=jnp.int32)
    pair = jnp.max(jnp.where(ordered[:, :, None] == nodes, (row // 2)[:, None, None], 0), axis=(0, 1))
    visit = (lax.rem(ordered // NC, NZ) * NZ + ordered // (NC * NZ) * NC + lax.rem(ordered, NC)).reshape(-1)
    spare = jnp.zeros((DIM - 2 * ROWS,), jnp.int32)
    table = jnp.stack([pair, visit, jnp.concatenate([order, place, spare])])
    return jnp.concatenate([table, jnp.zeros((5, DIM), jnp.int32)], axis=0)


def shards(queries, kv_cache, node_len, paths):
    rows, width = queries.shape
    meta = plan(paths)
    bf16, f32, i32 = jnp.bfloat16, jnp.float32, jnp.int32
    dma = pltpu.SemaphoreType.DMA
    vmem, smem = pl.BlockSpec(memory_space=pltpu.VMEM), pl.BlockSpec(memory_space=pltpu.SMEM)
    out = pl.pallas_call(
        kernel,
        out_shape=jax.ShapeDtypeStruct((OWN, NX * GROUP, DIM), bf16),
        in_specs=[vmem, pl.BlockSpec(memory_space=pl.ANY), vmem, smem, smem],
        out_specs=vmem,
        scratch_shapes=[
            pltpu.VMEM((ROWS, GROUP, DIM), bf16),
            pltpu.VMEM((PAIRS, 2 * GROUP, DIM), bf16),
            pltpu.VMEM((NZ, PAIRS, 2 * GROUP, DIM), bf16),
            pltpu.VMEM((PLANE, 2, TOKENS, DIM), bf16),
            pltpu.VMEM((PLANE, 8, DIM), i32),
            pltpu.VMEM((PLANE, TOKENS), f32),
            pltpu.VMEM((NZ, 8, DIM), i32),
            pltpu.SMEM((NZ, 8, DIM), i32),
            pltpu.VMEM((2, PLANE + 1, 2 * GROUP, DIM), f32),
            pltpu.VMEM((2, PLANE + 1, 2 * GROUP, DIM), f32),
            pltpu.VMEM((2, PLANE + 1, 2 * GROUP, DIM), f32),
            pltpu.VMEM((2, ROWS, GROUP, DIM), f32),
            pltpu.VMEM((2, 2, GROUP, DIM), f32),
            pltpu.VMEM((2, 2, FAR, HALF, GROUP, DIM), bf16),
            pltpu.VMEM((2, 2, FAR, HALF, GROUP, DIM), bf16),
            pltpu.VMEM((2, 2, FAR, GROUP, DIM), f32),
            pltpu.VMEM((2, 2, FAR, GROUP, DIM), f32),
            pltpu.VMEM((ROWS, GROUP, DIM), bf16),
            pltpu.VMEM((ROWS, GROUP, DIM), bf16),
            dma((NX,)), dma((NX,)),
            dma((2 * NY,)), dma((2 * NY,)),
            dma((2 * NY,)), dma((2 * NY,)),
            dma((2, 2, FAR)), dma((2, 2, FAR)),
            dma((2, FAR)), dma((2, FAR)),
            dma((NZ,)),
            dma((2, 2, FAR)), dma((2, 2, FAR)),
            dma((2, 2, FAR)), dma((2, 2, FAR)),
            dma((NX,)), dma((NX,)),
            dma((3,)),
        ],
        compiler_params=pltpu.CompilerParams(
            collective_id=0, has_side_effects=True, vmem_limit_bytes=40 * 1024 * 1024),
        cost_estimate=pl.CostEstimate(flops=1 << 30, bytes_accessed=1 << 22, transcendentals=1 << 21),
    )(queries.reshape(rows, NX * GROUP, DIM), kv_cache, meta, meta, node_len)
    return out.reshape(rows, width)


def solution(mesh):
    return jax.shard_map(
        shards,
        mesh=mesh,
        in_specs=(
            P(("node", "head"), None),
            P(None, "node", None, "head"),
            P("node"),
            P("node", None),
        ),
        out_specs=P(("node", "head"), None),
        check_vma=False,
    )
```

```python
import math

import jax
import jax.numpy as jnp
from jax import lax
from jax.experimental import pallas as pl
from jax.experimental.pallas import tpu as pltpu
from jax.sharding import PartitionSpec as P

MESH = pl.DeviceIdType.MESH
NX, NY, NZ, NC = 4, 4, 16, 2
PLANE = NY * NC
FAR = NZ // 2
ROWS, GROUP, DIM, TOKENS, DEPTH = 32, 16, 128, 512, 4
PAIRS = ROWS // 2
PAIR = 2 * GROUP
OWN = ROWS // NX
SUB = 8
EMPTY = -1e30
SCALE = math.log2(math.e) / math.sqrt(DIM)
WARM = 6
PER = 2 * (FAR + 1)


def ring_slot(side, hop):
    return hop if side == 0 else lax.rem(NZ - hop, NZ)


def kernel(
    q_ref, kv_ref, meta_ref, meta_s, len_s, out_ref,
    qx, qplane, kvz, lens, metav, metas, o_out, o_in, s_out, s_in, fin, fx,
    x_send, x_recv, kv_send, kv_recv, ln_send, ln_recv, q_send, q_recv, m_send, m_recv,
    ms_sem, o_send, o_recv, s_send, s_recv, r_send, r_recv, own_sem,
):
    node = lax.axis_index("node")
    x = lax.axis_index("head")
    core = lax.rem(node, NC)
    z = lax.rem(node // NC, NZ)
    y = node // (NC * NZ)

    def dev(yy, zz, cc, xx):
        return ((yy * NZ + zz) * NC + cc, xx)

    z_dev = (dev(y, lax.rem(z + 1, NZ), core, x), dev(y, lax.rem(z + NZ - 1, NZ), core, x))
    x_dev = [None] + [dev(y, z, core, lax.rem(x + d, NX)) for d in range(1, NX)]
    p_dev = [dev(lax.rem(y + j // NC, NY), z, lax.rem(core + j % NC, NC), x) for j in range(PLANE)]
    b_dev = [dev(lax.rem(y + NY - j // NC, NY), z, lax.rem(core + j % NC, NC), x) for j in range(PLANE)]

    barrier = pltpu.get_barrier_semaphore()
    partners = list(z_dev) + x_dev[1:] + p_dev[1:]
    for partner in partners:
        pl.semaphore_signal(barrier, inc=1, device_id=partner, device_id_type=MESH)
    pl.semaphore_wait(barrier, len(partners))

    def remote(src, dst, send, recv, to):
        return pltpu.make_async_remote_copy(
            src_ref=src, dst_ref=dst, send_sem=send, recv_sem=recv, device_id=to, device_id_type=MESH)

    def x_copy(d):
        heads = pl.ds(pl.multiple_of(lax.rem(x + d, NX) * GROUP, GROUP), GROUP)
        rows = pl.ds(pl.multiple_of(x * OWN, OWN), OWN)
        if d == 0:
            return pltpu.make_async_copy(q_ref.at[:, heads, :], qx.at[rows], own_sem.at[0])
        return remote(q_ref.at[:, heads, :], qx.at[rows], x_send.at[d], x_recv.at[d], x_dev[d])

    for d in (2, 1, 3, 0):
        x_copy(d).start()

    def first_kv(side, part):
        return remote(kv_ref.at[part, 0], kvz.at[ring_slot(side, 1), part], kv_send.at[side, part, 0],
                      kv_recv.at[side, part, 0], z_dev[side])

    def kv_copy(side, part, hop):
        return remote(kvz.at[ring_slot(side, hop - 1), part], kvz.at[ring_slot(side, hop), part],
                      kv_send.at[side, part, hop - 1], kv_recv.at[side, part, hop - 1], z_dev[side])

    def ln_copy(side, hop):
        return remote(lens.at[ring_slot(side, hop - 1)], lens.at[ring_slot(side, hop)],
                      ln_send.at[side, hop - 1], ln_recv.at[side, hop - 1], z_dev[side])

    lens[0] = jnp.full(lens.shape[1:], len_s[0], jnp.int32)
    for part in (0, 1):
        for side in (0, 1):
            first_kv(side, part).start()
        if part == 0:
            for side in (0, 1):
                ln_copy(side, 1).start()
    kv_own = [pltpu.make_async_copy(kv_ref.at[part, 0], kvz.at[0, part], own_sem.at[1 + part]) for part in (0, 1)]
    for copy in kv_own:
        copy.start()

    x_copy(0).wait()
    for d in (1, 3, 2):
        x_copy(d).wait_recv()
    for p in range(ROWS):
        qplane[0, p // 2, (p % 2) * GROUP:(p % 2 + 1) * GROUP, :] = qx[meta_s[2, p]]

    def q_copies(j):
        return (
            remote(qplane.at[0], qplane.at[j], q_send.at[j], q_recv.at[j], p_dev[j]),
            remote(meta_ref, metav.at[j], m_send.at[j], m_recv.at[j], p_dev[j]),
        )

    for j in (4, 5, 2, 3, 6, 7, 1):
        for copy in q_copies(j):
            copy.start()

    def m_local(j):
        src = meta_ref if j == 0 else metav.at[j]
        return pltpu.make_async_copy(src, metas.at[j], ms_sem.at[j])

    m_local(0).start()

    def relay(hop, part):
        for side in (0, 1):
            reach = FAR - 1 + (part + side + 1) % 2

            @pl.when(hop <= reach)
            def _(side=side):
                kv_copy(side, part, hop).wait_recv()

            @pl.when(hop < reach)
            def _(side=side):
                kv_copy(side, part, hop + 1).start()

            @pl.when((part == 0) & (hop <= FAR - side))
            def _(side=side):
                ln_copy(side, hop).wait_recv()

            @pl.when((part == 0) & (hop < FAR - side))
            def _(side=side):
                ln_copy(side, hop + 1).start()

    lane = lax.broadcasted_iota(jnp.int32, (SUB, DIM), 1)
    token = lax.broadcasted_iota(jnp.int32, (1, TOKENS), 1)

    def attend(i, hop, side):
        n = (y * NZ + lax.rem(z + NZ - i, NZ)) * NC + core
        length = jnp.concatenate([lens[i, 0:1, :]] * (TOKENS // DIM), axis=1)
        bias = jnp.where(token < length, 0.0, EMPTY)
        for j0 in range(0, PLANE, 4):
            lhs = jnp.concatenate([qplane[j, metas[j, 0, n]] for j in range(j0, j0 + 4)], axis=0)
            score = lax.dot_general(lhs, kvz[i, 0], (((1,), (1,)), ((), ())),
                                    preferred_element_type=jnp.float32) + bias
            peak = jnp.max(score, axis=1, keepdims=True)
            prob = jnp.exp2((score - peak) * SCALE)
            total = jnp.sum(prob, axis=1, keepdims=True)
            value = jnp.dot(prob.astype(jnp.bfloat16), kvz[i, 1],
                            preferred_element_type=jnp.float32).astype(jnp.bfloat16)
            for j in range(j0, j0 + 4):
                base = (j - j0) * PAIR
                at = j * PER + 2 * hop + side
                stat = jnp.zeros((SUB, DIM), jnp.float32)
                for c in range(PAIR // SUB):
                    rows = slice(base + c * SUB, base + (c + 1) * SUB)
                    stat = jnp.where(lane == c, peak[rows], stat)
                    stat = jnp.where(lane == c + PAIR // SUB, total[rows], stat)
                (o_in if j == 0 else o_out)[at] = value[base:base + PAIR]
                (s_in if j == 0 else s_out)[at] = stat

    def back_copies(j, hop, count):
        at = pl.ds(j * PER + 2 * hop, count)
        return (
            remote(o_out.at[at], o_in.at[at], o_send.at[j, hop], o_recv.at[j, hop], b_dev[j]),
            remote(s_out.at[at], s_in.at[at], s_send.at[j, hop], s_recv.at[j, hop], b_dev[j]),
        )

    for u in range(WARM):
        relay(u // 2 + 1, u % 2)
    for j in range(1, PLANE):
        for copy in q_copies(j):
            copy.wait_recv()
        m_local(j).start()
    for copy in kv_own:
        copy.wait()
    for j in range(PLANE):
        m_local(j).wait()

    def half_hop(u, carry):
        relay(u // 2 + 1, lax.rem(u, 2))
        hop = u - WARM
        attend(hop, hop, 0)
        attend(lax.rem(NZ - hop, NZ), hop, 1)
        for j in range(1, PLANE):
            for copy in back_copies(j, hop, 2):
                copy.start()
        return carry

    lax.fori_loop(WARM, WARM + FAR, half_hop, 0)
    for u in range(WARM + FAR, 2 * FAR):
        relay(u // 2 + 1, u % 2)
    attend(FAR, FAR, 0)
    for j in (4, 5, 2, 3, 6, 7, 1):
        for copy in back_copies(j, FAR, 1):
            copy.start()

    for hop in range(FAR + 1):
        for j in range(1, PLANE):
            for copy in back_copies(j, hop, 2 if hop < FAR else 1):
                copy.wait_recv()

    def column(tile, c):
        return jnp.concatenate(
            [jnp.broadcast_to(tile[:, c + h:c + h + 1], (SUB, DIM)) for h in range(GROUP // SUB)], axis=0)

    for p in range(ROWS):
        s = p % 2
        at = [meta_s[1, p * DEPTH + j] for j in range(DEPTH)]
        stats = [s_in[a] for a in at]
        peaks = [column(t, 2 * s) for t in stats]
        totals = [column(t, 2 * s + PAIR // SUB) for t in stats]
        top = jnp.maximum(jnp.maximum(peaks[0], peaks[1]), jnp.maximum(peaks[2], peaks[3]))
        total = jnp.zeros((GROUP, DIM), jnp.float32)
        value = jnp.zeros((GROUP, DIM), jnp.float32)
        for a, peak, t in zip(at, peaks, totals):
            weight = jnp.exp2((peak - top) * SCALE)
            total = total + weight * t
            value = value + weight * o_in[a, s * GROUP:(s + 1) * GROUP, :].astype(jnp.float32)
        fin[p] = (value / total).astype(jnp.bfloat16)

    for r in range(ROWS):
        fx[r] = fin[meta_s[2, ROWS + r]]

    def r_copy(d):
        rows = pl.ds(pl.multiple_of(lax.rem(x + d, NX) * OWN, OWN), OWN)
        heads = pl.ds(pl.multiple_of(x * GROUP, GROUP), GROUP)
        if d == 0:
            return pltpu.make_async_copy(fx.at[rows], out_ref.at[:, heads, :], own_sem.at[3])
        return remote(fx.at[rows], out_ref.at[:, heads, :], r_send.at[d], r_recv.at[d], x_dev[d])

    for d in (2, 1, 3, 0):
        r_copy(d).start()
    for d in (1, 2, 3):
        x_copy(d).wait_send()
    for side in (0, 1):
        for part in (0, 1):
            first_kv(side, part).wait_send()
            for hop in range(2, FAR + (1 if side == part else 0)):
                kv_copy(side, part, hop).wait_send()
        for hop in range(1, FAR + 1 - side):
            ln_copy(side, hop).wait_send()
    for j in range(1, PLANE):
        for copy in q_copies(j):
            copy.wait_send()
        for hop in range(FAR + 1):
            for copy in back_copies(j, hop, 2 if hop < FAR else 1):
                copy.wait_send()
    r_copy(0).wait()
    for d in (1, 3, 2):
        r_copy(d).wait()


def plan(paths):
    node, row = lax.axis_index("node"), jnp.arange(ROWS, dtype=jnp.int32)
    core, z, y = lax.rem(node, NC), lax.rem(node // NC, NZ), node // (NC * NZ)
    key = paths[:, 0] * ROWS + row
    place = jnp.sum((key[None, :] < key[:, None]).astype(jnp.int32), axis=1)
    at = (place[None, :] == row[:, None]).astype(jnp.int32)
    order = jnp.sum(at * row[None, :], axis=1)
    ordered = jnp.sum(at[:, :, None] * paths[None, :, :], axis=1)
    nodes = jnp.arange(PLANE * NZ, dtype=jnp.int32)
    pair = jnp.max(jnp.where(ordered[:, :, None] == nodes, (row // 2)[:, None, None], 0), axis=(0, 1))
    its_core, its_z, its_y = lax.rem(ordered, NC), lax.rem(ordered // NC, NZ), ordered // (NC * NZ)
    partner = lax.rem(its_y - y + NY, NY) * NC + lax.rem(its_core + core, NC)
    hop = lax.rem(z - its_z + NZ, NZ)
    visit = partner * PER + jnp.where(hop <= FAR, 2 * hop, 2 * (NZ - hop) + 1)
    spare = jnp.zeros((DIM - 2 * ROWS,), jnp.int32)
    table = jnp.stack([pair, visit.reshape(-1), jnp.concatenate([order, place, spare])])
    return jnp.concatenate([table, jnp.zeros((5, DIM), jnp.int32)], axis=0)


def shards(queries, kv_cache, node_len, paths):
    rows, width = queries.shape
    meta = plan(paths)
    bf16, f32, i32 = jnp.bfloat16, jnp.float32, jnp.int32
    dma = pltpu.SemaphoreType.DMA
    vmem, smem = pl.BlockSpec(memory_space=pltpu.VMEM), pl.BlockSpec(memory_space=pltpu.SMEM)
    out = pl.pallas_call(
        kernel,
        out_shape=jax.ShapeDtypeStruct((OWN, NX * GROUP, DIM), bf16),
        in_specs=[vmem, pl.BlockSpec(memory_space=pl.ANY), vmem, smem, smem],
        out_specs=vmem,
        scratch_shapes=[
            pltpu.VMEM((ROWS, GROUP, DIM), bf16),
            pltpu.VMEM((PLANE, PAIRS, PAIR, DIM), bf16),
            pltpu.VMEM((NZ, 2, TOKENS, DIM), bf16),
            pltpu.VMEM((NZ, SUB, DIM), i32),
            pltpu.VMEM((PLANE, SUB, DIM), i32),
            pltpu.SMEM((PLANE, SUB, DIM), i32),
            pltpu.VMEM((PLANE * PER, PAIR, DIM), bf16),
            pltpu.VMEM((PLANE * PER, PAIR, DIM), bf16),
            pltpu.VMEM((PLANE * PER, SUB, DIM), f32),
            pltpu.VMEM((PLANE * PER, SUB, DIM), f32),
            pltpu.VMEM((ROWS, GROUP, DIM), bf16),
            pltpu.VMEM((ROWS, GROUP, DIM), bf16),
            dma((NX,)), dma((NX,)),
            dma((2, 2, FAR)), dma((2, 2, FAR)),
            dma((2, FAR)), dma((2, FAR)),
            dma((PLANE,)), dma((PLANE,)),
            dma((PLANE,)), dma((PLANE,)),
            dma((PLANE,)),
            dma((PLANE, FAR + 1)), dma((PLANE, FAR + 1)),
            dma((PLANE, FAR + 1)), dma((PLANE, FAR + 1)),
            dma((NX,)), dma((NX,)),
            dma((4,)),
        ],
        compiler_params=pltpu.CompilerParams(
            collective_id=0, has_side_effects=True, vmem_limit_bytes=40 * 1024 * 1024),
        cost_estimate=pl.CostEstimate(flops=1 << 30, bytes_accessed=1 << 22, transcendentals=1 << 21),
    )(queries.reshape(rows, NX * GROUP, DIM), kv_cache, meta, meta, node_len)
    return out.reshape(rows, width)


def solution(mesh):
    return jax.shard_map(
        shards,
        mesh=mesh,
        in_specs=(
            P(("node", "head"), None),
            P(None, "node", None, "head"),
            P("node"),
            P("node", None),
        ),
        out_specs=P(("node", "head"), None),
        check_vma=False,
    )
```

```python
import math

import jax
import jax.numpy as jnp
from jax import lax
from jax.experimental import pallas as pl
from jax.experimental.pallas import tpu as pltpu
from jax.sharding import PartitionSpec as P

MESH = pl.DeviceIdType.MESH
NX, NY, NZ, NC = 4, 4, 16, 2
PLANE = NY * NC
FAR = NZ // 2
ROWS, GROUP, DIM, TOKENS, DEPTH = 32, 16, 128, 512, 4
PAIRS = ROWS // 2
PAIR = 2 * GROUP
OWN = ROWS // NX
LANES = GROUP * DIM
SUB = 8
EMPTY = -1e30
SCALE = math.log2(math.e) / math.sqrt(DIM)
CHUNKS = 4
CHUNK = 2 * TOKENS // CHUNKS
HEAD = 16
WARM = 3
BATCH = 4
SPAN = PLANE * BATCH


def ring_slot(side, hop):
    return hop if side == 0 else lax.rem(NZ - hop, NZ)


def reach(side, chunk):
    return FAR if side == chunk % 2 else FAR - 1


def chunk_rows(chunk):
    if isinstance(chunk, int) and chunk == 0:
        return pl.ds(0, HEAD + CHUNK)
    return pl.ds(pl.multiple_of(HEAD + chunk * CHUNK, 16), CHUNK)


def kernel(
    q_ref, kv_ref, len_ref, paths_ref, out_ref,
    qx, qf, qn, qplane, kvz, len_v, paths_v, metav, metas, o_out, o_in, s_out, s_in, ff, fx,
    x_send, x_recv, kv_send, kv_recv, q_send, q_recv, m_send, m_recv,
    o_send, o_recv, s_send, s_recv, r_send, r_recv, own_sem,
):
    node = lax.axis_index("node")
    x = lax.axis_index("head")
    core = lax.rem(node, NC)
    z = lax.rem(node // NC, NZ)
    y = node // (NC * NZ)

    def dev(yy, zz, cc, xx):
        return ((yy * NZ + zz) * NC + cc, xx)

    z_dev = (dev(y, lax.rem(z + 1, NZ), core, x), dev(y, lax.rem(z + NZ - 1, NZ), core, x))
    x_dev = [None] + [dev(y, z, core, lax.rem(x + d, NX)) for d in range(1, NX)]
    p_dev = [dev(lax.rem(y + j // NC, NY), z, lax.rem(core + j % NC, NC), x) for j in range(PLANE)]
    b_dev = [dev(lax.rem(y + NY - j // NC, NY), z, lax.rem(core + j % NC, NC), x) for j in range(PLANE)]

    barrier = pltpu.get_barrier_semaphore()
    partners = list(z_dev) + x_dev[1:] + p_dev[1:]
    for partner in partners:
        pl.semaphore_signal(barrier, inc=1, device_id=partner, device_id_type=MESH)

    kv_own = [pltpu.make_async_copy(kv_ref.at[part, 0], kvz.at[0, pl.ds(HEAD + part * TOKENS, TOKENS)],
                                    own_sem.at[part]) for part in (0, 1)]
    small = [pltpu.make_async_copy(len_ref, len_v, own_sem.at[2]),
             pltpu.make_async_copy(paths_ref, paths_v, own_sem.at[3])]
    for copy in kv_own + small:
        copy.start()
    small[0].wait()
    length = jnp.broadcast_to(len_v[...], (HEAD, DIM))
    upper = lax.broadcasted_iota(jnp.int32, (HEAD, DIM), 0) < HEAD // 2
    kvz[0, 0:HEAD, :] = jnp.where(upper, length >> 8, length & 255).astype(jnp.float32).astype(jnp.bfloat16)
    for copy in kv_own:
        copy.wait()
    pl.semaphore_wait(barrier, len(partners))

    def remote(src, dst, send, recv, to):
        return pltpu.make_async_remote_copy(
            src_ref=src, dst_ref=dst, send_sem=send, recv_sem=recv, device_id=to, device_id_type=MESH)

    def kv_copy(side, chunk, hop):
        rows = chunk_rows(chunk)
        return remote(kvz.at[ring_slot(side, hop - 1), rows], kvz.at[ring_slot(side, hop), rows],
                      kv_send.at[side, chunk], kv_recv.at[side, chunk, hop - 1], z_dev[side])

    def x_copy(d):
        lanes = pl.ds(pl.multiple_of(lax.rem(x + d, NX) * LANES, LANES), LANES)
        if d == 0:
            return pltpu.make_async_copy(q_ref.at[:, lanes], qx.at[x], x_recv.at[0])
        return remote(q_ref.at[:, lanes], qx.at[x], x_send.at[0], x_recv.at[d], x_dev[d])

    for side in (0, 1):
        kv_copy(side, 0, 1).start()
    for d in (2, 1, 3, 0):
        x_copy(d).start()
    for chunk in range(1, CHUNKS):
        for side in (0, 1):
            kv_copy(side, chunk, 1).start()

    def relay(hop, chunk, far=False):
        for side in (0, 1):
            last = reach(side, chunk) if far else FAR
            if not far or hop <= last:
                kv_copy(side, chunk, hop).wait_recv()
            if not far or hop < last:
                kv_copy(side, chunk, hop).wait_send()
                kv_copy(side, chunk, hop + 1).start()

    small[1].wait()
    row = lax.broadcasted_iota(jnp.int32, (ROWS, DIM), 0)
    col = lax.broadcasted_iota(jnp.int32, (ROWS, DIM), 1)

    def upright(line):
        return jnp.sum(jnp.where(row == col, line, 0), axis=1, keepdims=True)

    wide = jnp.concatenate([paths_v[...], jnp.zeros((DEPTH, DIM - ROWS), jnp.int32)], axis=1)
    key_line = wide[0:1, :] * ROWS + col[0:1, :]
    key = upright(key_line)
    place_line = jnp.sum(jnp.where(key < key_line, 1, 0), axis=0, keepdims=True)
    place = upright(place_line)
    order_line = jnp.sum(jnp.where(place == col, row, 0), axis=0, keepdims=True)
    pair = jnp.zeros((ROWS, DIM), jnp.int32)
    for j in range(DEPTH):
        pair = jnp.maximum(pair, jnp.where(upright(wide[j:j + 1, :]) == col, place >> 1, 0))
    metav[0, 0:1, :] = jnp.max(pair, axis=0, keepdims=True)
    for j in range(DEPTH):
        n = wide[j:j + 1, :]
        partner = (((n >> 5) - y + NY) & (NY - 1)) * NC + (((n & 1) + core) & 1)
        hop = (z - ((n >> 1) & (NZ - 1)) + NZ) & (NZ - 1)
        t = jnp.where(hop == 0, 0, jnp.where(hop <= FAR, 2 * hop - 1, 2 * (NZ - hop)))
        at = (t >> 2) * SPAN + partner * BATCH + (t & 3)
        metav[0, 1 + j:2 + j, :] = at * 2 + (place_line & 1)
    metav[0, 5:6, :] = order_line
    metav[0, 6:8, :] = jnp.zeros((2, DIM), jnp.int32)
    own_meta = pltpu.make_async_copy(metav.at[0], metas.at[0], own_sem.at[4])
    own_meta.start()

    relay(1, 0)
    x_copy(0).wait()
    for d in (1, 3, 2):
        x_copy(d).wait_recv()
    for h in range(GROUP):
        for i in range(NX):
            qf[h * ROWS + i * OWN:h * ROWS + (i + 1) * OWN, :] = (
                qx[i, :, h * DIM:(h + 1) * DIM].astype(jnp.float32))
    relay(1, 1)
    for r in range(ROWS):
        qn[r] = qf[pl.ds(r, GROUP, stride=ROWS), :].astype(jnp.bfloat16)
    own_meta.wait()
    for p in range(ROWS):
        qplane[0, p // 2, (p % 2) * GROUP:(p % 2 + 1) * GROUP, :] = qn[metas[0, 5, p]]

    def q_copies(j, count=1):
        src = pl.ds(0, count)
        return (
            remote(qplane.at[src], qplane.at[pl.ds(j, count)], q_send.at[0], q_recv.at[0], p_dev[j]),
            remote(metav.at[src], metav.at[pl.ds(j, count)], m_send.at[0], m_recv.at[0], p_dev[j]),
        )

    for j in (4, 5, 2, 3, 6, 7, 1):
        for copy in q_copies(j):
            copy.start()

    lane = lax.broadcasted_iota(jnp.int32, (SUB, DIM), 1)
    token = lax.broadcasted_iota(jnp.int32, (1, TOKENS), 1).astype(jnp.float32)

    def ring_of(t):
        odd = lax.rem(t, 2)
        return odd * ((t + 1) // 2) + (1 - odd) * lax.rem(NZ - t // 2, NZ)

    def scores(t, j0):
        i = ring_of(t)
        n = (y * NZ + lax.rem(z + NZ - i, NZ)) * NC + core
        head = kvz[i, 0:HEAD, :].astype(jnp.float32)
        length = head[0:1, :] * 256.0 + head[HEAD // 2:HEAD // 2 + 1, :]
        bias = jnp.where(token < jnp.concatenate([length] * (TOKENS // DIM), axis=1), 0.0, EMPTY)
        lhs = jnp.concatenate([qplane[j, metas[j, 0, n]] for j in range(j0, j0 + 4)], axis=0)
        score = lax.dot_general(lhs, kvz[i, pl.ds(HEAD, TOKENS), :], (((1,), (1,)), ((), ())),
                                preferred_element_type=jnp.float32) + bias
        peak = jnp.max(score, axis=1, keepdims=True)
        prob = jnp.exp2((score - peak) * SCALE)
        return prob.astype(jnp.bfloat16), peak, jnp.sum(prob, axis=1, keepdims=True)

    def values(t, j0, prob, peak, total):
        i = ring_of(t)
        value = jnp.dot(prob, kvz[i, pl.ds(HEAD + TOKENS, TOKENS), :],
                        preferred_element_type=jnp.float32).astype(jnp.bfloat16)
        for j in range(j0, j0 + 4):
            base = (j - j0) * PAIR
            at = t // BATCH * SPAN + j * BATCH + lax.rem(t, BATCH)
            stat = jnp.zeros((SUB, DIM), jnp.float32)
            for c in range(PAIR // SUB):
                rows = slice(base + c * SUB, base + (c + 1) * SUB)
                stat = jnp.where(lane == c, peak[rows], stat)
                stat = jnp.where(lane == c + PAIR // SUB, total[rows], stat)
            for c in range(2):
                (o_in if j == 0 else o_out)[2 * at + c] = value[base + c * GROUP:base + (c + 1) * GROUP]
            (s_in if j == 0 else s_out)[at] = stat

    def attend(t):
        for j0 in (0, 4):
            values(t, j0, *scores(t, j0))

    def back_copies(j, b, first, count):
        at = pl.ds(b * SPAN + j * BATCH + first, count)
        both = pl.ds(2 * (b * SPAN + j * BATCH + first), 2 * count)
        return (
            remote(o_out.at[both], o_in.at[both], o_send.at[b], o_recv.at[b], b_dev[j]),
            remote(s_out.at[at], s_in.at[at], s_send.at[b], s_recv.at[b], b_dev[j]),
        )

    def send(b, first, count, partners=range(1, PLANE)):
        for j in partners:
            for copy in back_copies(j, b, first, count):
                copy.start()

    def all_copies(b):
        return back_copies(1, b, 0, SPAN - BATCH)

    for chunk in range(2, CHUNKS):
        relay(1, chunk)
    for hop in range(2, WARM + 1):
        for chunk in range(CHUNKS):
            relay(hop, chunk)
    for copy in q_copies(1, PLANE - 1):
        copy.wait_recv()
    all_meta = pltpu.make_async_copy(metav.at[pl.ds(1, PLANE - 1)], metas.at[pl.ds(1, PLANE - 1)], own_sem.at[5])
    all_meta.start()
    all_meta.wait()

    def one_hop(b, carry):
        hop = WARM + 1 + b

        def one_chunk(chunk, carry):
            @pl.when(chunk == 0)
            def _():
                relay(hop, 0)

            @pl.when(chunk > 0)
            def _():
                relay(hop, chunk)

            attend(BATCH * b + chunk)
            return carry

        lax.fori_loop(0, CHUNKS, one_chunk, 0)
        send(b, 0, BATCH)

        @pl.when(b >= 1)
        def _():
            for copy in all_copies(b - 1):
                copy.wait()

        return carry

    lax.fori_loop(0, 3, one_hop, 0)
    for chunk in range(CHUNKS):
        relay(FAR - 1, chunk, True)
        if chunk == 0:
            attend(12)
            for copy in all_copies(2):
                copy.wait()
    attend(13)
    relay(FAR, 0, True)
    attend(14)
    send(3, 0, 3)
    relay(FAR, 1, True)
    last = [(j0, scores(15, j0)) for j0 in (4, 0)]
    relay(FAR, 2, True)
    relay(FAR, 3, True)
    for j0, found in last:
        values(15, j0, *found)
        send(3, 3, 1, range(max(j0, 1), j0 + 4))
    for copy in all_copies(3):
        copy.wait_recv()

    def finish(r):
        at = [metas[0, 1 + j, r] for j in range(DEPTH)]
        stats = []
        for a in at:
            tile = s_in[a // 2]
            stats.append(jnp.where(a % 2 == 1, pltpu.roll(tile, DIM - 2, 1), tile))
        top = jnp.maximum(jnp.maximum(stats[0], stats[1]), jnp.maximum(stats[2], stats[3]))
        weight = [jnp.exp2((t - top) * SCALE) for t in stats]
        total = sum(pltpu.roll(w, PAIR // SUB, 1) * t for w, t in zip(weight, stats))
        share = pltpu.roll(1.0 / jnp.where(lane < PAIR // SUB, 1.0, total), DIM - PAIR // SUB, 1)
        value = jnp.zeros((GROUP, DIM), jnp.float32)
        for a, w in zip(at, weight):
            w = w * share
            w = jnp.concatenate([jnp.broadcast_to(w[:, c:c + 1], (SUB, DIM)) for c in range(GROUP // SUB)], axis=0)
            value = value + w * o_in[a].astype(jnp.float32)
        return value

    def r_copy(d):
        lanes = pl.ds(pl.multiple_of(x * LANES, LANES), LANES)
        if d == 0:
            return pltpu.make_async_copy(fx.at[0], out_ref.at[:, lanes], r_recv.at[0])
        return remote(fx.at[d], out_ref.at[:, lanes], r_send.at[0], r_recv.at[d], x_dev[d])

    for d in (2, 1, 3, 0):
        for r in range(OWN):
            ff[d, pl.ds(r, GROUP, stride=OWN), :] = finish(lax.rem(x + d, NX) * OWN + r)
        for h in range(GROUP):
            fx[d, :, h * DIM:(h + 1) * DIM] = ff[d, h * OWN:(h + 1) * OWN, :].astype(jnp.bfloat16)
        r_copy(d).start()
    for d in (1, 2, 3):
        x_copy(d).wait_send()
    for side in (0, 1):
        for chunk in range(CHUNKS):
            kv_copy(side, chunk, reach(side, chunk)).wait_send()
    for copy in q_copies(1, PLANE - 1) + all_copies(3):
        copy.wait_send()
    r_copy(0).wait()
    for d in (1, 3, 2):
        r_copy(d).wait()


def shards(queries, kv_cache, node_len, paths):
    rows, width = queries.shape
    bf16, f32, i32 = jnp.bfloat16, jnp.float32, jnp.int32
    dma = pltpu.SemaphoreType.DMA
    anywhere = pl.BlockSpec(memory_space=pl.ANY)
    return pl.pallas_call(
        kernel,
        out_shape=jax.ShapeDtypeStruct((rows, width), bf16),
        in_specs=[anywhere] * 4,
        out_specs=anywhere,
        scratch_shapes=[
            pltpu.VMEM((NX, OWN, LANES), bf16),
            pltpu.VMEM((GROUP * ROWS, DIM), f32),
            pltpu.VMEM((ROWS, GROUP, DIM), bf16),
            pltpu.VMEM((PLANE, PAIRS, PAIR, DIM), bf16),
            pltpu.VMEM((NZ, HEAD + 2 * TOKENS, DIM), bf16),
            pltpu.VMEM((1, 1), i32),
            pltpu.VMEM((DEPTH, ROWS), i32),
            pltpu.VMEM((PLANE, SUB, DIM), i32),
            pltpu.SMEM((PLANE, SUB, DIM), i32),
            pltpu.VMEM((2 * PLANE * NZ, GROUP, DIM), bf16),
            pltpu.VMEM((2 * PLANE * NZ, GROUP, DIM), bf16),
            pltpu.VMEM((PLANE * NZ, SUB, DIM), f32),
            pltpu.VMEM((PLANE * NZ, SUB, DIM), f32),
            pltpu.VMEM((NX, GROUP * OWN, DIM), f32),
            pltpu.VMEM((NX, OWN, LANES), bf16),
            dma((1,)), dma((NX,)),
            dma((2, CHUNKS)), dma((2, CHUNKS, FAR)),
            dma((1,)), dma((1,)),
            dma((1,)), dma((1,)),
            dma((NZ // BATCH,)), dma((NZ // BATCH,)),
            dma((NZ // BATCH,)), dma((NZ // BATCH,)),
            dma((1,)), dma((NX,)),
            dma((6,)),
        ],
        compiler_params=pltpu.CompilerParams(
            collective_id=0, has_side_effects=True, vmem_limit_bytes=60 * 1024 * 1024),
        cost_estimate=pl.CostEstimate(flops=1 << 30, bytes_accessed=1 << 22, transcendentals=1 << 21),
    )(queries, kv_cache, node_len.reshape(1, 1), paths.T)


def solution(mesh):
    return jax.shard_map(
        shards,
        mesh=mesh,
        in_specs=(
            P(("node", "head"), None),
            P(None, "node", None, "head"),
            P("node"),
            P("node", None),
        ),
        out_specs=P(("node", "head"), None),
        check_vma=False,
    )
```

```python
import math

import jax
import jax.numpy as jnp
from jax import lax
from jax.experimental import pallas as pl
from jax.experimental.pallas import tpu as pltpu
from jax.sharding import PartitionSpec as P

MESH = pl.DeviceIdType.MESH
NX, NY, NZ, NC = 4, 4, 16, 2
PLANE = NY * NC
FAR = NZ // 2
ROWS, GROUP, DIM, TOKENS, DEPTH = 32, 16, 128, 512, 4
PAIRS = ROWS // 2
PAIR = 2 * GROUP
OWN = ROWS // NX
LANES = GROUP * DIM
SUB = 8
EMPTY = -1e30
SCALE = math.log2(math.e) / math.sqrt(DIM)
CHUNKS = 4
CHUNK = 2 * TOKENS // CHUNKS
HEAD = 16
WARM = 3
BATCH = 4
SPAN = PLANE * BATCH


def ring_slot(side, hop):
    return hop if side == 0 else lax.rem(NZ - hop, NZ)


def reach(side, chunk):
    return FAR if side == chunk % 2 else FAR - 1


def chunk_rows(chunk):
    if isinstance(chunk, int) and chunk == 0:
        return pl.ds(0, HEAD + CHUNK)
    return pl.ds(pl.multiple_of(HEAD + chunk * CHUNK, 16), CHUNK)


def kernel(
    q_ref, kv_ref, len_ref, paths_ref, out_ref,
    qx, qf, qn, qplane, kvz, len_v, paths_v, metav, metas, o_out, o_in, s_out, s_in, ff, fx,
    x_send, x_recv, kv_send, kv_recv, q_send, q_recv, m_send, m_recv,
    o_send, o_recv, s_send, s_recv, r_send, r_recv, own_sem,
):
    node = lax.axis_index("node")
    x = lax.axis_index("head")
    core = lax.rem(node, NC)
    z = lax.rem(node // NC, NZ)
    y = node // (NC * NZ)

    def dev(yy, zz, cc, xx):
        return ((yy * NZ + zz) * NC + cc, xx)

    z_dev = (dev(y, lax.rem(z + 1, NZ), core, x), dev(y, lax.rem(z + NZ - 1, NZ), core, x))
    x_dev = [None] + [dev(y, z, core, lax.rem(x + d, NX)) for d in range(1, NX)]
    p_dev = [dev(lax.rem(y + j // NC, NY), z, lax.rem(core + j % NC, NC), x) for j in range(PLANE)]
    b_dev = [dev(lax.rem(y + NY - j // NC, NY), z, lax.rem(core + j % NC, NC), x) for j in range(PLANE)]

    barrier = pltpu.get_barrier_semaphore()
    partners = list(z_dev) + x_dev[1:] + p_dev[1:]
    for partner in partners:
        pl.semaphore_signal(barrier, inc=1, device_id=partner, device_id_type=MESH)

    kv_own = [pltpu.make_async_copy(kv_ref.at[part, 0], kvz.at[0, pl.ds(HEAD + part * TOKENS, TOKENS)],
                                    own_sem.at[part]) for part in (0, 1)]
    small = [pltpu.make_async_copy(len_ref, len_v, own_sem.at[2]),
             pltpu.make_async_copy(paths_ref, paths_v, own_sem.at[3])]
    for copy in kv_own + small:
        copy.start()
    small[0].wait()
    length = jnp.broadcast_to(len_v[...], (HEAD, DIM))
    upper = lax.broadcasted_iota(jnp.int32, (HEAD, DIM), 0) < HEAD // 2
    kvz[0, 0:HEAD, :] = jnp.where(upper, length >> 8, length & 255).astype(jnp.float32).astype(jnp.bfloat16)
    for copy in kv_own:
        copy.wait()
    pl.semaphore_wait(barrier, len(partners))

    def remote(src, dst, send, recv, to):
        return pltpu.make_async_remote_copy(
            src_ref=src, dst_ref=dst, send_sem=send, recv_sem=recv, device_id=to, device_id_type=MESH)

    def kv_copy(side, chunk, hop):
        rows = chunk_rows(chunk)
        return remote(kvz.at[ring_slot(side, hop - 1), rows], kvz.at[ring_slot(side, hop), rows],
                      kv_send.at[side, chunk], kv_recv.at[side, chunk, hop - 1], z_dev[side])

    def x_copy(d):
        lanes = pl.ds(pl.multiple_of(lax.rem(x + d, NX) * LANES, LANES), LANES)
        if d == 0:
            return pltpu.make_async_copy(q_ref.at[:, lanes], qx.at[x], x_recv.at[0])
        return remote(q_ref.at[:, lanes], qx.at[x], x_send.at[0], x_recv.at[d], x_dev[d])

    for side in (0, 1):
        kv_copy(side, 0, 1).start()
    for d in (2, 1, 3, 0):
        x_copy(d).start()
    for chunk in range(1, CHUNKS):
        for side in (0, 1):
            kv_copy(side, chunk, 1).start()

    def relay(hop, chunk, far=False):
        for side in (0, 1):
            last = reach(side, chunk) if far else FAR
            if not far or hop <= last:
                kv_copy(side, chunk, hop).wait_recv()
            if not far or hop < last:
                kv_copy(side, chunk, hop).wait_send()
                kv_copy(side, chunk, hop + 1).start()

    small[1].wait()
    row = lax.broadcasted_iota(jnp.int32, (ROWS, DIM), 0)
    col = lax.broadcasted_iota(jnp.int32, (ROWS, DIM), 1)

    def upright(line):
        return jnp.sum(jnp.where(row == col, line, 0), axis=1, keepdims=True)

    level = [paths_v[:, j:j + 1] for j in range(DEPTH)]
    key = level[0] * ROWS + row[:, 0:1]
    key_line = jnp.sum(jnp.where(row == col, key, 0), axis=0, keepdims=True)
    place_line = jnp.sum(jnp.where(key < key_line, 1, 0), axis=0, keepdims=True)
    place = upright(place_line)
    order_line = jnp.sum(jnp.where(place == col, row, 0), axis=0, keepdims=True)
    pair = jnp.zeros((ROWS, DIM), jnp.int32)
    for j in range(DEPTH):
        pair = jnp.maximum(pair, jnp.where(level[j] == col, place >> 1, 0))
    metav[0, 0:1, :] = jnp.max(pair, axis=0, keepdims=True)
    for j in range(DEPTH):
        n = jnp.sum(jnp.where(row == col, level[j], 0), axis=0, keepdims=True)
        partner = (((n >> 5) - y + NY) & (NY - 1)) * NC + (((n & 1) + core) & 1)
        hop = (z - ((n >> 1) & (NZ - 1)) + NZ) & (NZ - 1)
        t = jnp.where(hop == 0, 0, jnp.where(hop <= FAR, 2 * hop - 1, 2 * (NZ - hop)))
        at = (t >> 2) * SPAN + partner * BATCH + (t & 3)
        metav[0, 1 + j:2 + j, :] = at * 2 + (place_line & 1)
    metav[0, 5:6, :] = order_line
    metav[0, 6:8, :] = jnp.zeros((2, DIM), jnp.int32)
    own_meta = pltpu.make_async_copy(metav.at[0], metas.at[0], own_sem.at[4])
    own_meta.start()

    relay(1, 0)
    x_copy(0).wait()
    for d in (1, 3, 2):
        x_copy(d).wait_recv()
    for h in range(GROUP):
        for i in range(NX):
            qf[h * ROWS + i * OWN:h * ROWS + (i + 1) * OWN, :] = (
                qx[i, :, h * DIM:(h + 1) * DIM].astype(jnp.float32))
    relay(1, 1)
    for r in range(ROWS):
        qn[r] = qf[pl.ds(r, GROUP, stride=ROWS), :].astype(jnp.bfloat16)
    own_meta.wait()
    for p in range(ROWS):
        qplane[0, p // 2, (p % 2) * GROUP:(p % 2 + 1) * GROUP, :] = qn[metas[0, 5, p]]

    def q_copies(j, count=1):
        src = pl.ds(0, count)
        return (
            remote(qplane.at[src], qplane.at[pl.ds(j, count)], q_send.at[0], q_recv.at[0], p_dev[j]),
            remote(metav.at[src], metav.at[pl.ds(j, count)], m_send.at[0], m_recv.at[0], p_dev[j]),
        )

    for j in (4, 5, 2, 3, 6, 7, 1):
        for copy in q_copies(j):
            copy.start()

    lane = lax.broadcasted_iota(jnp.int32, (SUB, DIM), 1)
    token = lax.broadcasted_iota(jnp.int32, (1, TOKENS), 1).astype(jnp.float32)

    def ring_of(t):
        odd = lax.rem(t, 2)
        return odd * ((t + 1) // 2) + (1 - odd) * lax.rem(NZ - t // 2, NZ)

    def scores(t, j0):
        i = ring_of(t)
        n = (y * NZ + lax.rem(z + NZ - i, NZ)) * NC + core
        head = kvz[i, 0:HEAD, :].astype(jnp.float32)
        length = head[0:1, :] * 256.0 + head[HEAD // 2:HEAD // 2 + 1, :]
        bias = jnp.where(token < jnp.concatenate([length] * (TOKENS // DIM), axis=1), 0.0, EMPTY)
        lhs = jnp.concatenate([qplane[j, metas[j, 0, n]] for j in range(j0, j0 + 4)], axis=0)
        score = lax.dot_general(lhs, kvz[i, pl.ds(HEAD, TOKENS), :], (((1,), (1,)), ((), ())),
                                preferred_element_type=jnp.float32) + bias
        peak = jnp.max(score, axis=1, keepdims=True)
        prob = jnp.exp2((score - peak) * SCALE)
        return prob.astype(jnp.bfloat16), peak, jnp.sum(prob, axis=1, keepdims=True)

    def values(t, j0, prob, peak, total):
        i = ring_of(t)
        value = jnp.dot(prob, kvz[i, pl.ds(HEAD + TOKENS, TOKENS), :],
                        preferred_element_type=jnp.float32).astype(jnp.bfloat16)
        for j in range(j0, j0 + 4):
            base = (j - j0) * PAIR
            at = t // BATCH * SPAN + j * BATCH + lax.rem(t, BATCH)
            stat = jnp.zeros((SUB, DIM), jnp.float32)
            for c in range(PAIR // SUB):
                rows = slice(base + c * SUB, base + (c + 1) * SUB)
                stat = jnp.where(lane == c, peak[rows], stat)
                stat = jnp.where(lane == c + PAIR // SUB, total[rows], stat)
            for c in range(2):
                (o_in if j == 0 else o_out)[2 * at + c] = value[base + c * GROUP:base + (c + 1) * GROUP]
            (s_in if j == 0 else s_out)[at] = stat

    def attend(t):
        for j0 in (0, 4):
            values(t, j0, *scores(t, j0))

    def back_copies(j, b, first, count):
        at = pl.ds(b * SPAN + j * BATCH + first, count)
        both = pl.ds(2 * (b * SPAN + j * BATCH + first), 2 * count)
        return (
            remote(o_out.at[both], o_in.at[both], o_send.at[b], o_recv.at[b], b_dev[j]),
            remote(s_out.at[at], s_in.at[at], s_send.at[b], s_recv.at[b], b_dev[j]),
        )

    def send(b, first, count, partners=range(1, PLANE)):
        for j in partners:
            for copy in back_copies(j, b, first, count):
                copy.start()

    def all_copies(b):
        return back_copies(1, b, 0, SPAN - BATCH)

    for chunk in range(2, CHUNKS):
        relay(1, chunk)
    for hop in range(2, WARM + 1):
        for chunk in range(CHUNKS):
            relay(hop, chunk)
    relay(WARM + 1, 0)
    for copy in q_copies(1, PLANE - 1):
        copy.wait_recv()
    all_meta = pltpu.make_async_copy(metav.at[pl.ds(1, PLANE - 1)], metas.at[pl.ds(1, PLANE - 1)], own_sem.at[5])
    all_meta.start()
    all_meta.wait()

    def one_hop(b, carry):
        hop = WARM + 1 + b

        def one_chunk(q, carry):
            @pl.when((q >= 1) & (q < CHUNKS))
            def _():
                relay(hop, q)

            attend(BATCH * b + q)
            return carry

        lax.fori_loop(0, CHUNKS, one_chunk, 0)

        @pl.when(b < 2)
        def _():
            relay(hop + 1, 0)

        send(b, 0, BATCH)

        return carry

    lax.fori_loop(0, 3, one_hop, 0)
    relay(FAR - 1, 0, True)
    attend(12)
    relay(FAR - 1, 1, True)
    found = [(t, j0, scores(t, j0)) for t in (13, 14) for j0 in (0, 4)]
    relay(FAR - 1, 2, True)
    relay(FAR - 1, 3, True)
    for t, j0, parts in found:
        values(t, j0, *parts)
    send(3, 0, 3)
    relay(FAR, 0, True)
    relay(FAR, 1, True)
    found = [(j0, scores(15, j0)) for j0 in (4, 0)]
    relay(FAR, 2, True)
    relay(FAR, 3, True)
    for j0, parts in found:
        values(15, j0, *parts)
        send(3, 3, 1, range(max(j0, 1), j0 + 4))
    for b in range(3):
        for copy in all_copies(b):
            copy.wait()
    for copy in all_copies(3):
        copy.wait_recv()

    def finish(r):
        at = [metas[0, 1 + j, r] for j in range(DEPTH)]
        stats = []
        for a in at:
            tile = s_in[a // 2]
            stats.append(jnp.where(a % 2 == 1, pltpu.roll(tile, DIM - 2, 1), tile))
        top = jnp.maximum(jnp.maximum(stats[0], stats[1]), jnp.maximum(stats[2], stats[3]))
        weight = [jnp.exp2((t - top) * SCALE) for t in stats]
        total = sum(pltpu.roll(w, PAIR // SUB, 1) * t for w, t in zip(weight, stats))
        share = pltpu.roll(1.0 / jnp.where(lane < PAIR // SUB, 1.0, total), DIM - PAIR // SUB, 1)
        value = jnp.zeros((GROUP, DIM), jnp.float32)
        for a, w in zip(at, weight):
            w = w * share
            w = jnp.concatenate([jnp.broadcast_to(w[:, c:c + 1], (SUB, DIM)) for c in range(GROUP // SUB)], axis=0)
            value = value + w * o_in[a].astype(jnp.float32)
        return value

    def r_copy(d):
        lanes = pl.ds(pl.multiple_of(x * LANES, LANES), LANES)
        if d == 0:
            return pltpu.make_async_copy(fx.at[0], out_ref.at[:, lanes], r_recv.at[0])
        return remote(fx.at[d], out_ref.at[:, lanes], r_send.at[0], r_recv.at[d], x_dev[d])

    for d in (2, 1, 3, 0):
        for r in range(OWN):
            ff[d, pl.ds(r, GROUP, stride=OWN), :] = finish(lax.rem(x + d, NX) * OWN + r)
        for h in range(GROUP):
            fx[d, :, h * DIM:(h + 1) * DIM] = ff[d, h * OWN:(h + 1) * OWN, :].astype(jnp.bfloat16)
        r_copy(d).start()
    for d in (1, 2, 3):
        x_copy(d).wait_send()
    for side in (0, 1):
        for chunk in range(CHUNKS):
            kv_copy(side, chunk, reach(side, chunk)).wait_send()
    for copy in q_copies(1, PLANE - 1) + all_copies(3):
        copy.wait_send()
    r_copy(0).wait()
    for d in (1, 3, 2):
        r_copy(d).wait()


def shards(queries, kv_cache, node_len, paths):
    rows, width = queries.shape
    bf16, f32, i32 = jnp.bfloat16, jnp.float32, jnp.int32
    dma = pltpu.SemaphoreType.DMA
    anywhere = pl.BlockSpec(memory_space=pl.ANY)
    return pl.pallas_call(
        kernel,
        out_shape=jax.ShapeDtypeStruct((rows, width), bf16),
        in_specs=[anywhere] * 4,
        out_specs=anywhere,
        scratch_shapes=[
            pltpu.VMEM((NX, OWN, LANES), bf16),
            pltpu.VMEM((GROUP * ROWS, DIM), f32),
            pltpu.VMEM((ROWS, GROUP, DIM), bf16),
            pltpu.VMEM((PLANE, PAIRS, PAIR, DIM), bf16),
            pltpu.VMEM((NZ, HEAD + 2 * TOKENS, DIM), bf16),
            pltpu.VMEM((1, 1), i32),
            pltpu.VMEM((ROWS, DEPTH), i32),
            pltpu.VMEM((PLANE, SUB, DIM), i32),
            pltpu.SMEM((PLANE, SUB, DIM), i32),
            pltpu.VMEM((2 * PLANE * NZ, GROUP, DIM), bf16),
            pltpu.VMEM((2 * PLANE * NZ, GROUP, DIM), bf16),
            pltpu.VMEM((PLANE * NZ, SUB, DIM), f32),
            pltpu.VMEM((PLANE * NZ, SUB, DIM), f32),
            pltpu.VMEM((NX, GROUP * OWN, DIM), f32),
            pltpu.VMEM((NX, OWN, LANES), bf16),
            dma((1,)), dma((NX,)),
            dma((2, CHUNKS)), dma((2, CHUNKS, FAR)),
            dma((1,)), dma((1,)),
            dma((1,)), dma((1,)),
            dma((NZ // BATCH,)), dma((NZ // BATCH,)),
            dma((NZ // BATCH,)), dma((NZ // BATCH,)),
            dma((1,)), dma((NX,)),
            dma((6,)),
        ],
        compiler_params=pltpu.CompilerParams(
            collective_id=0, has_side_effects=True, vmem_limit_bytes=56356864),
        cost_estimate=pl.CostEstimate(flops=1 << 30, bytes_accessed=1 << 22, transcendentals=1 << 21),
    )(queries, kv_cache, node_len.reshape(1, 1), paths)


def solution(mesh):
    return jax.shard_map(
        shards,
        mesh=mesh,
        in_specs=(
            P(("node", "head"), None),
            P(None, "node", None, "head"),
            P("node"),
            P("node", None),
        ),
        out_specs=P(("node", "head"), None),
        check_vma=False,
    )
```

```python
import math

import jax
import jax.numpy as jnp
from jax import lax
from jax.experimental import pallas as pl
from jax.experimental.pallas import tpu as pltpu
from jax.sharding import PartitionSpec as P

MESH = pl.DeviceIdType.MESH
NX, NY, NZ, NC = 4, 4, 16, 2
PLANE = NY * NC
FAR = NZ // 2
ROWS, GROUP, DIM, TOKENS, DEPTH = 32, 16, 128, 512, 4
PAIRS = ROWS // 2
PAIR = 2 * GROUP
OWN = ROWS // NX
LANES = GROUP * DIM
SUB = 8
EMPTY = -1e30
SCALE = math.log2(math.e) / math.sqrt(DIM)
CHUNKS = 4
CHUNK = 2 * TOKENS // CHUNKS
HEAD = 16
WARM = 3
BATCH = 4
SPAN = PLANE * BATCH


def ring_slot(side, hop):
    return hop if side == 0 else lax.rem(NZ - hop, NZ)


def reach(side, chunk):
    return FAR if side == chunk % 2 else FAR - 1


def chunk_rows(chunk):
    if isinstance(chunk, int) and chunk == 0:
        return pl.ds(0, HEAD + CHUNK)
    return pl.ds(pl.multiple_of(HEAD + chunk * CHUNK, 16), CHUNK)


def kernel(
    q_ref, kv_ref, len_ref, paths_ref, out_ref,
    qx, qf, qn, qplane, kvz, len_v, paths_v, metav, metas, o_out, o_in, s_out, s_in, ff, fx,
    x_send, x_recv, kv_send, kv_recv, q_send, q_recv, m_send, m_recv,
    o_send, o_recv, s_send, s_recv, r_send, r_recv, own_sem,
):
    node = lax.axis_index("node")
    x = lax.axis_index("head")
    core = lax.rem(node, NC)
    z = lax.rem(node // NC, NZ)
    y = node // (NC * NZ)

    def dev(yy, zz, cc, xx):
        return ((yy * NZ + zz) * NC + cc, xx)

    z_dev = (dev(y, lax.rem(z + 1, NZ), core, x), dev(y, lax.rem(z + NZ - 1, NZ), core, x))
    x_dev = [None] + [dev(y, z, core, lax.rem(x + d, NX)) for d in range(1, NX)]
    p_dev = [dev(lax.rem(y + j // NC, NY), z, lax.rem(core + j % NC, NC), x) for j in range(PLANE)]
    b_dev = [dev(lax.rem(y + NY - j // NC, NY), z, lax.rem(core + j % NC, NC), x) for j in range(PLANE)]

    barrier = pltpu.get_barrier_semaphore()
    partners = list(z_dev) + x_dev[1:] + p_dev[1:]
    for partner in partners:
        pl.semaphore_signal(barrier, inc=1, device_id=partner, device_id_type=MESH)

    kv_own = [pltpu.make_async_copy(kv_ref.at[part, 0], kvz.at[0, pl.ds(HEAD + part * TOKENS, TOKENS)],
                                    own_sem.at[part]) for part in (0, 1)]
    small = [pltpu.make_async_copy(len_ref, len_v, own_sem.at[2]),
             pltpu.make_async_copy(paths_ref, paths_v, own_sem.at[3])]
    for copy in kv_own + small:
        copy.start()
    small[0].wait()
    length = jnp.broadcast_to(len_v[...], (HEAD, DIM))
    upper = lax.broadcasted_iota(jnp.int32, (HEAD, DIM), 0) < HEAD // 2
    kvz[0, 0:HEAD, :] = jnp.where(upper, length >> 8, length & 255).astype(jnp.float32).astype(jnp.bfloat16)
    for copy in kv_own:
        copy.wait()
    pl.semaphore_wait(barrier, len(partners))

    def remote(src, dst, send, recv, to):
        return pltpu.make_async_remote_copy(
            src_ref=src, dst_ref=dst, send_sem=send, recv_sem=recv, device_id=to, device_id_type=MESH)

    def kv_copy(side, chunk, hop):
        rows = chunk_rows(chunk)
        return remote(kvz.at[ring_slot(side, hop - 1), rows], kvz.at[ring_slot(side, hop), rows],
                      kv_send.at[side, chunk], kv_recv.at[side, chunk, hop - 1], z_dev[side])

    def x_copy(d):
        lanes = pl.ds(pl.multiple_of(lax.rem(x + d, NX) * LANES, LANES), LANES)
        if d == 0:
            return pltpu.make_async_copy(q_ref.at[:, lanes], qx.at[x], x_recv.at[0])
        return remote(q_ref.at[:, lanes], qx.at[x], x_send.at[0], x_recv.at[d], x_dev[d])

    def chunk_of(side, step):
        return step ^ side

    for side in (0, 1):
        kv_copy(side, chunk_of(side, 0), 1).start()
    for d in (2, 1, 3, 0):
        x_copy(d).start()
    for step in range(1, CHUNKS):
        for side in (0, 1):
            kv_copy(side, chunk_of(side, step), 1).start()

    def relay(hop, step, far=False):
        for side in (0, 1):
            chunk = chunk_of(side, step)
            last = reach(side, chunk) if far else FAR
            if not far or hop <= last:
                kv_copy(side, chunk, hop).wait_recv()
            if not far or hop < last:
                kv_copy(side, chunk, hop).wait_send()
                kv_copy(side, chunk, hop + 1).start()

    small[1].wait()
    row = lax.broadcasted_iota(jnp.int32, (ROWS, DIM), 0)
    col = lax.broadcasted_iota(jnp.int32, (ROWS, DIM), 1)

    def upright(line):
        return jnp.sum(jnp.where(row == col, line, 0), axis=1, keepdims=True)

    level = [paths_v[:, j:j + 1] for j in range(DEPTH)]
    key = level[0] * ROWS + row[:, 0:1]
    key_line = jnp.sum(jnp.where(row == col, key, 0), axis=0, keepdims=True)
    place_line = jnp.sum(jnp.where(key < key_line, 1, 0), axis=0, keepdims=True)
    place = upright(place_line)
    order_line = jnp.sum(jnp.where(place == col, row, 0), axis=0, keepdims=True)
    pair = jnp.zeros((ROWS, DIM), jnp.int32)
    for j in range(DEPTH):
        pair = jnp.maximum(pair, jnp.where(level[j] == col, place >> 1, 0))
    metav[0, 0:1, :] = jnp.max(pair, axis=0, keepdims=True)
    for j in range(DEPTH):
        n = jnp.sum(jnp.where(row == col, level[j], 0), axis=0, keepdims=True)
        partner = (((n >> 5) - y + NY) & (NY - 1)) * NC + (((n & 1) + core) & 1)
        hop = (z - ((n >> 1) & (NZ - 1)) + NZ) & (NZ - 1)
        t = jnp.where(hop == 0, 0, jnp.where(hop <= FAR, 2 * hop - 1, 2 * (NZ - hop)))
        at = (t >> 2) * SPAN + partner * BATCH + (t & 3)
        metav[0, 1 + j:2 + j, :] = at * 2 + (place_line & 1)
    metav[0, 5:6, :] = order_line
    metav[0, 6:8, :] = jnp.zeros((2, DIM), jnp.int32)
    own_meta = pltpu.make_async_copy(metav.at[0], metas.at[0], own_sem.at[4])
    own_meta.start()

    relay(1, 0)
    x_copy(0).wait()
    for d in (1, 3, 2):
        x_copy(d).wait_recv()
    for h in range(GROUP):
        for i in range(NX):
            qf[h * ROWS + i * OWN:h * ROWS + (i + 1) * OWN, :] = (
                qx[i, :, h * DIM:(h + 1) * DIM].astype(jnp.float32))
    relay(1, 1)
    for r in range(ROWS):
        qn[r] = qf[pl.ds(r, GROUP, stride=ROWS), :].astype(jnp.bfloat16)
    own_meta.wait()
    for p in range(ROWS):
        qplane[0, p // 2, (p % 2) * GROUP:(p % 2 + 1) * GROUP, :] = qn[metas[0, 5, p]]

    def q_copies(j, count=1):
        src = pl.ds(0, count)
        return (
            remote(qplane.at[src], qplane.at[pl.ds(j, count)], q_send.at[0], q_recv.at[0], p_dev[j]),
            remote(metav.at[src], metav.at[pl.ds(j, count)], m_send.at[0], m_recv.at[0], p_dev[j]),
        )

    for j in (4, 5, 2, 3, 6, 7, 1):
        for copy in q_copies(j):
            copy.start()

    lane = lax.broadcasted_iota(jnp.int32, (SUB, DIM), 1)
    token = lax.broadcasted_iota(jnp.int32, (1, TOKENS), 1).astype(jnp.float32)

    def ring_of(t):
        odd = lax.rem(t, 2)
        return odd * ((t + 1) // 2) + (1 - odd) * lax.rem(NZ - t // 2, NZ)

    def scores(t, j0):
        i = ring_of(t)
        n = (y * NZ + lax.rem(z + NZ - i, NZ)) * NC + core
        head = kvz[i, 0:HEAD, :].astype(jnp.float32)
        length = head[0:1, :] * 256.0 + head[HEAD // 2:HEAD // 2 + 1, :]
        bias = jnp.where(token < jnp.concatenate([length] * (TOKENS // DIM), axis=1), 0.0, EMPTY)
        lhs = jnp.concatenate([qplane[j, metas[j, 0, n]] for j in range(j0, j0 + 4)], axis=0)
        score = lax.dot_general(lhs, kvz[i, pl.ds(HEAD, TOKENS), :], (((1,), (1,)), ((), ())),
                                preferred_element_type=jnp.float32) + bias
        peak = jnp.max(score, axis=1, keepdims=True)
        prob = jnp.exp2((score - peak) * SCALE)
        return prob.astype(jnp.bfloat16), peak, jnp.sum(prob, axis=1, keepdims=True)

    def values(t, j0, prob, peak, total):
        i = ring_of(t)
        value = jnp.dot(prob, kvz[i, pl.ds(HEAD + TOKENS, TOKENS), :],
                        preferred_element_type=jnp.float32).astype(jnp.bfloat16)
        for j in range(j0, j0 + 4):
            base = (j - j0) * PAIR
            at = t // BATCH * SPAN + j * BATCH + lax.rem(t, BATCH)
            stat = jnp.zeros((SUB, DIM), jnp.float32)
            for c in range(PAIR // SUB):
                rows = slice(base + c * SUB, base + (c + 1) * SUB)
                stat = jnp.where(lane == c, peak[rows], stat)
                stat = jnp.where(lane == c + PAIR // SUB, total[rows], stat)
            for c in range(2):
                (o_in if j == 0 else o_out)[2 * at + c] = value[base + c * GROUP:base + (c + 1) * GROUP]
            (s_in if j == 0 else s_out)[at] = stat

    def attend(t):
        for j0 in (0, 4):
            values(t, j0, *scores(t, j0))

    def back_copies(j, b, first, count):
        at = pl.ds(b * SPAN + j * BATCH + first, count)
        both = pl.ds(2 * (b * SPAN + j * BATCH + first), 2 * count)
        return (
            remote(o_out.at[both], o_in.at[both], o_send.at[b], o_recv.at[b], b_dev[j]),
            remote(s_out.at[at], s_in.at[at], s_send.at[b], s_recv.at[b], b_dev[j]),
        )

    def send(b, first, count, partners=range(1, PLANE)):
        for j in partners:
            for copy in back_copies(j, b, first, count):
                copy.start()

    def all_copies(b):
        return back_copies(1, b, 0, SPAN - BATCH)

    for chunk in range(2, CHUNKS):
        relay(1, chunk)
    for hop in range(2, WARM + 1):
        for chunk in range(CHUNKS):
            relay(hop, chunk)
    relay(WARM + 1, 0)
    for copy in q_copies(1, PLANE - 1):
        copy.wait_recv()
    all_meta = pltpu.make_async_copy(metav.at[pl.ds(1, PLANE - 1)], metas.at[pl.ds(1, PLANE - 1)], own_sem.at[5])
    all_meta.start()
    all_meta.wait()

    def one_hop(b, carry):
        hop = WARM + 1 + b

        def one_chunk(q, carry):
            for step in range(1, CHUNKS):
                @pl.when(q == step)
                def _(step=step):
                    relay(hop, step)

            attend(BATCH * b + q)
            return carry

        lax.fori_loop(0, CHUNKS, one_chunk, 0)

        @pl.when(b < 2)
        def _():
            relay(hop + 1, 0)

        send(b, 0, BATCH)

        return carry

    lax.fori_loop(0, 3, one_hop, 0)
    relay(FAR - 1, 0, True)
    attend(12)
    relay(FAR - 1, 1, True)
    found = [(t, j0, scores(t, j0)) for t in (13, 14) for j0 in (0, 4)]
    relay(FAR - 1, 2, True)
    relay(FAR - 1, 3, True)
    for t, j0, parts in found:
        values(t, j0, *parts)
    send(3, 0, 3)
    relay(FAR, 0, True)
    found = [(j0, scores(15, j0)) for j0 in (4, 0)]
    relay(FAR, 2, True)
    for j0, parts in found:
        values(15, j0, *parts)
        send(3, 3, 1, range(max(j0, 1), j0 + 4))
    for b in range(3):
        for copy in all_copies(b):
            copy.wait()
    for copy in all_copies(3):
        copy.wait_recv()

    def finish(r):
        at = [metas[0, 1 + j, r] for j in range(DEPTH)]
        stats = []
        for a in at:
            tile = s_in[a // 2]
            stats.append(jnp.where(a % 2 == 1, pltpu.roll(tile, DIM - 2, 1), tile))
        top = jnp.maximum(jnp.maximum(stats[0], stats[1]), jnp.maximum(stats[2], stats[3]))
        weight = [jnp.exp2((t - top) * SCALE) for t in stats]
        total = sum(pltpu.roll(w, PAIR // SUB, 1) * t for w, t in zip(weight, stats))
        share = pltpu.roll(1.0 / jnp.where(lane < PAIR // SUB, 1.0, total), DIM - PAIR // SUB, 1)
        value = jnp.zeros((GROUP, DIM), jnp.float32)
        for a, w in zip(at, weight):
            w = w * share
            w = jnp.concatenate([jnp.broadcast_to(w[:, c:c + 1], (SUB, DIM)) for c in range(GROUP // SUB)], axis=0)
            value = value + w * o_in[a].astype(jnp.float32)
        return value

    def r_copy(d):
        lanes = pl.ds(pl.multiple_of(x * LANES, LANES), LANES)
        if d == 0:
            return pltpu.make_async_copy(fx.at[0], out_ref.at[:, lanes], r_recv.at[0])
        return remote(fx.at[d], out_ref.at[:, lanes], r_send.at[0], r_recv.at[d], x_dev[d])

    for d in (2, 1, 3, 0):
        for r in range(OWN):
            ff[d, pl.ds(r, GROUP, stride=OWN), :] = finish(lax.rem(x + d, NX) * OWN + r)
        for h in range(GROUP):
            fx[d, :, h * DIM:(h + 1) * DIM] = ff[d, h * OWN:(h + 1) * OWN, :].astype(jnp.bfloat16)
        r_copy(d).start()
    for d in (1, 2, 3):
        x_copy(d).wait_send()
    for side in (0, 1):
        for chunk in range(CHUNKS):
            kv_copy(side, chunk, reach(side, chunk)).wait_send()
    for copy in q_copies(1, PLANE - 1) + all_copies(3):
        copy.wait_send()
    r_copy(0).wait()
    for d in (1, 3, 2):
        r_copy(d).wait()


def shards(queries, kv_cache, node_len, paths):
    rows, width = queries.shape
    bf16, f32, i32 = jnp.bfloat16, jnp.float32, jnp.int32
    dma = pltpu.SemaphoreType.DMA
    anywhere = pl.BlockSpec(memory_space=pl.ANY)
    return pl.pallas_call(
        kernel,
        out_shape=jax.ShapeDtypeStruct((rows, width), bf16),
        in_specs=[anywhere] * 4,
        out_specs=anywhere,
        scratch_shapes=[
            pltpu.VMEM((NX, OWN, LANES), bf16),
            pltpu.VMEM((GROUP * ROWS, DIM), f32),
            pltpu.VMEM((ROWS, GROUP, DIM), bf16),
            pltpu.VMEM((PLANE, PAIRS, PAIR, DIM), bf16),
            pltpu.VMEM((NZ, HEAD + 2 * TOKENS, DIM), bf16),
            pltpu.VMEM((1, 1), i32),
            pltpu.VMEM((ROWS, DEPTH), i32),
            pltpu.VMEM((PLANE, SUB, DIM), i32),
            pltpu.SMEM((PLANE, SUB, DIM), i32),
            pltpu.VMEM((2 * PLANE * NZ, GROUP, DIM), bf16),
            pltpu.VMEM((2 * PLANE * NZ, GROUP, DIM), bf16),
            pltpu.VMEM((PLANE * NZ, SUB, DIM), f32),
            pltpu.VMEM((PLANE * NZ, SUB, DIM), f32),
            pltpu.VMEM((NX, GROUP * OWN, DIM), f32),
            pltpu.VMEM((NX, OWN, LANES), bf16),
            dma((1,)), dma((NX,)),
            dma((2, CHUNKS)), dma((2, CHUNKS, FAR)),
            dma((1,)), dma((1,)),
            dma((1,)), dma((1,)),
            dma((NZ // BATCH,)), dma((NZ // BATCH,)),
            dma((NZ // BATCH,)), dma((NZ // BATCH,)),
            dma((1,)), dma((NX,)),
            dma((6,)),
        ],
        compiler_params=pltpu.CompilerParams(
            collective_id=0, has_side_effects=True, vmem_limit_bytes=56356864),
        cost_estimate=pl.CostEstimate(flops=1 << 30, bytes_accessed=1 << 22, transcendentals=1 << 21),
    )(queries, kv_cache, node_len.reshape(1, 1), paths)


def solution(mesh):
    return jax.shard_map(
        shards,
        mesh=mesh,
        in_specs=(
            P(("node", "head"), None),
            P(None, "node", None, "head"),
            P("node"),
            P("node", None),
        ),
        out_specs=P(("node", "head"), None),
        check_vma=False,
    )
```

```python
import math

import jax
import jax.numpy as jnp
from jax import lax
from jax.experimental import pallas as pl
from jax.experimental.pallas import tpu as pltpu
from jax.sharding import PartitionSpec as P

MESH = pl.DeviceIdType.MESH
NX, NY, NZ, NC = 4, 4, 16, 2
PLANE = NY * NC
FAR = NZ // 2
ROWS, GROUP, DIM, TOKENS, DEPTH = 32, 16, 128, 512, 4
PAIRS = ROWS // 2
PAIR = 2 * GROUP
OWN = ROWS // NX
LANES = GROUP * DIM
SUB = 8
EMPTY = -1e30
SCALE = math.log2(math.e) / math.sqrt(DIM)
CHUNKS = 4
CHUNK = 2 * TOKENS // CHUNKS
HEAD = 16
VALUES = TOKENS + HEAD
WARM = 3
BATCH = 4
SPAN = PLANE * BATCH


def ring_slot(side, hop):
    return hop if side == 0 else lax.rem(NZ - hop, NZ)


def reach(side, chunk):
    return FAR if side == chunk % 2 else FAR - 1


def chunk_rows(chunk):
    if isinstance(chunk, int):
        return pl.ds(chunk * CHUNK + (HEAD if chunk > 1 else 0), CHUNK + (HEAD if chunk == 1 else 0))
    return pl.ds(pl.multiple_of(HEAD + chunk * CHUNK, 16), CHUNK)


def kernel(
    q_ref, kv_ref, len_ref, paths_ref, out_ref,
    qx, qf, qn, qplane, kvz, len_v, paths_v, metav, metas, o_out, o_in, s_out, s_in, ff, fx,
    x_send, x_recv, kv_send, kv_recv, q_send, q_recv, m_send, m_recv,
    o_send, o_recv, s_send, s_recv, r_send, r_recv, own_sem,
):
    node = lax.axis_index("node")
    x = lax.axis_index("head")
    core = lax.rem(node, NC)
    z = lax.rem(node // NC, NZ)
    y = node // (NC * NZ)

    def dev(yy, zz, cc, xx):
        return ((yy * NZ + zz) * NC + cc, xx)

    z_dev = (dev(y, lax.rem(z + 1, NZ), core, x), dev(y, lax.rem(z + NZ - 1, NZ), core, x))
    x_dev = [None] + [dev(y, z, core, lax.rem(x + d, NX)) for d in range(1, NX)]
    p_dev = [dev(lax.rem(y + j // NC, NY), z, lax.rem(core + j % NC, NC), x) for j in range(PLANE)]
    b_dev = [dev(lax.rem(y + NY - j // NC, NY), z, lax.rem(core + j % NC, NC), x) for j in range(PLANE)]

    barrier = pltpu.get_barrier_semaphore()
    partners = list(z_dev) + x_dev[1:] + p_dev[1:]
    for partner in partners:
        pl.semaphore_signal(barrier, inc=1, device_id=partner, device_id_type=MESH)

    kv_own = [pltpu.make_async_copy(kv_ref.at[part, 0], kvz.at[0, pl.ds(part * VALUES, TOKENS)],
                                    own_sem.at[part]) for part in (0, 1)]
    small = [pltpu.make_async_copy(len_ref, len_v, own_sem.at[2]),
             pltpu.make_async_copy(paths_ref, paths_v, own_sem.at[3])]
    for copy in small + kv_own:
        copy.start()
    pl.semaphore_wait(barrier, len(partners))

    def remote(src, dst, send, recv, to):
        return pltpu.make_async_remote_copy(
            src_ref=src, dst_ref=dst, send_sem=send, recv_sem=recv, device_id=to, device_id_type=MESH)

    def kv_copy(side, chunk, hop, first=False):
        rows = chunk_rows(chunk)
        if first:
            src = kv_ref.at[chunk // 2, 0, pl.ds(chunk % 2 * CHUNK, CHUNK)]
            return remote(src, kvz.at[ring_slot(side, 1), rows], kv_send.at[side, chunk],
                          kv_recv.at[chunk ^ side, 0], z_dev[side])
        return remote(kvz.at[ring_slot(side, hop - 1), rows], kvz.at[ring_slot(side, hop), rows],
                      kv_send.at[side, chunk], kv_recv.at[chunk ^ side, hop - 1], z_dev[side])

    def x_copy(d):
        lanes = pl.ds(pl.multiple_of(lax.rem(x + d, NX) * LANES, LANES), LANES)
        if d == 0:
            return pltpu.make_async_copy(q_ref.at[:, lanes], qx.at[x], x_recv.at[0])
        return remote(q_ref.at[:, lanes], qx.at[x], x_send.at[0], x_recv.at[d], x_dev[d])

    def chunk_of(side, step):
        return step ^ side

    kv_copy(0, 0, 1, True).start()
    for d in (2, 1, 3, 0):
        x_copy(d).start()
    small[0].wait()
    length = jnp.broadcast_to(len_v[...], (HEAD, DIM))
    upper = lax.broadcasted_iota(jnp.int32, (HEAD, DIM), 0) < HEAD // 2
    kvz[0, TOKENS:VALUES, :] = jnp.where(upper, length >> 8, length & 255).astype(jnp.float32).astype(jnp.bfloat16)
    kv_own[0].wait()
    kv_copy(1, 1, 1).start()
    for step in range(1, CHUNKS):
        for side in (0, 1):
            kv_copy(side, chunk_of(side, step), 1, chunk_of(side, step) != 1).start()

    def relay(hop, step, far=False):
        rows = pl.ds(0, 2 * CHUNK + (HEAD if step < 2 else 0))
        remote(kvz.at[1, rows], kvz.at[1, rows], kv_send.at[0, 0], kv_recv.at[step, hop - 1], z_dev[0]).wait_recv()
        for side in (0, 1):
            chunk = chunk_of(side, step)
            own = isinstance(hop, int) and hop == 1 and chunk != 1
            last = reach(side, chunk) if far else FAR
            if not far or hop < last:
                kv_copy(side, chunk, hop, own).wait_send()
                kv_copy(side, chunk, hop + 1).start()

    small[1].wait()
    row = lax.broadcasted_iota(jnp.int32, (ROWS, DIM), 0)
    col = lax.broadcasted_iota(jnp.int32, (ROWS, DIM), 1)

    def upright(line):
        return jnp.sum(jnp.where(row == col, line, 0), axis=1, keepdims=True)

    level = [paths_v[:, j:j + 1] for j in range(DEPTH)]
    key = level[0] * ROWS + row[:, 0:1]
    key_line = jnp.sum(jnp.where(row == col, key, 0), axis=0, keepdims=True)
    place_line = jnp.sum(jnp.where(key < key_line, 1, 0), axis=0, keepdims=True)
    place = upright(place_line)
    order_line = jnp.sum(jnp.where(place == col, row, 0), axis=0, keepdims=True)
    pair = jnp.zeros((ROWS, DIM), jnp.int32)
    for j in range(DEPTH):
        pair = jnp.maximum(pair, jnp.where(level[j] == col, place >> 1, 0))
    metav[0, 0:1, :] = jnp.max(pair, axis=0, keepdims=True)
    for j in range(DEPTH):
        n = jnp.sum(jnp.where(row == col, level[j], 0), axis=0, keepdims=True)
        partner = (((n >> 5) - y + NY) & (NY - 1)) * NC + (((n & 1) + core) & 1)
        hop = (z - ((n >> 1) & (NZ - 1)) + NZ) & (NZ - 1)
        t = jnp.where(hop == 0, 0, jnp.where(hop <= FAR, 2 * hop - 1, 2 * (NZ - hop)))
        at = (t >> 2) * SPAN + partner * BATCH + (t & 3)
        metav[0, 1 + j:2 + j, :] = at * 2 + (place_line & 1)
    metav[0, 5:6, :] = order_line
    metav[0, 6:8, :] = jnp.zeros((2, DIM), jnp.int32)
    own_meta = pltpu.make_async_copy(metav.at[0], metas.at[0], own_sem.at[4])
    own_meta.start()

    relay(1, 0)
    x_copy(0).wait()
    for d in (1, 3, 2):
        x_copy(d).wait_recv()
    for h in range(GROUP):
        for i in range(NX):
            qf[h * ROWS + i * OWN:h * ROWS + (i + 1) * OWN, :] = (
                qx[i, :, h * DIM:(h + 1) * DIM].astype(jnp.float32))
    relay(1, 1)
    for r in range(ROWS):
        qn[r] = qf[pl.ds(r, GROUP, stride=ROWS), :].astype(jnp.bfloat16)
    own_meta.wait()
    for p in range(ROWS):
        qplane[0, p // 2, (p % 2) * GROUP:(p % 2 + 1) * GROUP, :] = qn[metas[0, 5, p]]

    def q_copies(j, count=1):
        src = pl.ds(0, count)
        return (
            remote(qplane.at[src], qplane.at[pl.ds(j, count)], q_send.at[0], q_recv.at[0], p_dev[j]),
            remote(metav.at[src], metav.at[pl.ds(j, count)], m_send.at[0], m_recv.at[0], p_dev[j]),
        )

    for j in (4, 5, 2, 3, 6, 7, 1):
        for copy in q_copies(j):
            copy.start()

    lane = lax.broadcasted_iota(jnp.int32, (SUB, DIM), 1)
    token = lax.broadcasted_iota(jnp.int32, (1, TOKENS), 1).astype(jnp.float32)

    def ring_of(t):
        odd = lax.rem(t, 2)
        return odd * ((t + 1) // 2) + (1 - odd) * lax.rem(NZ - t // 2, NZ)

    def scores(t, j0):
        i = ring_of(t)
        n = (y * NZ + lax.rem(z + NZ - i, NZ)) * NC + core
        head = kvz[i, TOKENS:VALUES, :].astype(jnp.float32)
        length = head[0:1, :] * 256.0 + head[HEAD // 2:HEAD // 2 + 1, :]
        bias = jnp.where(token < jnp.concatenate([length] * (TOKENS // DIM), axis=1), 0.0, EMPTY)
        lhs = jnp.concatenate([qplane[j, metas[j, 0, n]] for j in range(j0, j0 + 4)], axis=0)
        score = lax.dot_general(lhs, kvz[i, 0:TOKENS, :], (((1,), (1,)), ((), ())),
                                preferred_element_type=jnp.float32) + bias
        peak = jnp.max(score, axis=1, keepdims=True)
        prob = jnp.exp2((score - peak) * SCALE)
        return prob.astype(jnp.bfloat16), peak, jnp.sum(prob, axis=1, keepdims=True)

    def values(t, j0, prob, peak, total):
        i = ring_of(t)
        value = jnp.dot(prob, kvz[i, VALUES:VALUES + TOKENS, :],
                        preferred_element_type=jnp.float32).astype(jnp.bfloat16)
        for j in range(j0, j0 + 4):
            base = (j - j0) * PAIR
            at = t // BATCH * SPAN + j * BATCH + lax.rem(t, BATCH)
            stat = jnp.zeros((SUB, DIM), jnp.float32)
            for c in range(PAIR // SUB):
                rows = slice(base + c * SUB, base + (c + 1) * SUB)
                stat = jnp.where(lane == c, peak[rows], stat)
                stat = jnp.where(lane == c + PAIR // SUB, total[rows], stat)
            for c in range(2):
                (o_in if j == 0 else o_out)[2 * at + c] = value[base + c * GROUP:base + (c + 1) * GROUP]
            (s_in if j == 0 else s_out)[at] = stat

    def attend(t):
        for j0 in (0, 4):
            values(t, j0, *scores(t, j0))

    def back_copies(j, b, first, count):
        at = pl.ds(b * SPAN + j * BATCH + first, count)
        both = pl.ds(2 * (b * SPAN + j * BATCH + first), 2 * count)
        return (
            remote(o_out.at[both], o_in.at[both], o_send.at[b], o_recv.at[b], b_dev[j]),
            remote(s_out.at[at], s_in.at[at], s_send.at[b], s_recv.at[b], b_dev[j]),
        )

    def send(b, first, count, partners=range(1, PLANE)):
        for j in partners:
            for copy in back_copies(j, b, first, count):
                copy.start()

    def all_copies(b):
        return back_copies(1, b, 0, SPAN - BATCH)

    kv_own[1].wait()
    for chunk in range(2, CHUNKS):
        relay(1, chunk)
    for hop in range(2, WARM + 1):
        for chunk in range(CHUNKS):
            relay(hop, chunk)
    relay(WARM + 1, 0)
    for copy in q_copies(1, PLANE - 1):
        copy.wait_recv()
    all_meta = pltpu.make_async_copy(metav.at[pl.ds(1, PLANE - 1)], metas.at[pl.ds(1, PLANE - 1)], own_sem.at[5])
    all_meta.start()
    all_meta.wait()

    def one_hop(b, carry):
        hop = WARM + 1 + b

        def one_chunk(q, carry):
            for step in range(1, CHUNKS):
                @pl.when(q == step)
                def _(step=step):
                    relay(hop, step)

            attend(BATCH * b + q)
            return carry

        lax.fori_loop(0, CHUNKS, one_chunk, 0)

        @pl.when(b < 2)
        def _():
            relay(hop + 1, 0)

        send(b, 0, BATCH)

        return carry

    lax.fori_loop(0, 3, one_hop, 0)
    relay(FAR - 1, 0, True)
    attend(12)
    relay(FAR - 1, 1, True)
    found = [(t, j0, scores(t, j0)) for t in (13, 14) for j0 in (0, 4)]
    relay(FAR - 1, 2, True)
    relay(FAR - 1, 3, True)
    for t, j0, parts in found:
        values(t, j0, *parts)
    send(3, 0, 3)
    relay(FAR, 0, True)
    found = [(j0, scores(15, j0)) for j0 in (4, 0)]
    relay(FAR, 2, True)
    for j0, parts in found:
        values(15, j0, *parts)
        send(3, 3, 1, range(max(j0, 1), j0 + 4))
    for b in range(3):
        for copy in all_copies(b):
            copy.wait()
    for copy in all_copies(3):
        copy.wait_recv()

    def finish(r):
        at = [metas[0, 1 + j, r] for j in range(DEPTH)]
        stats = []
        for a in at:
            tile = s_in[a // 2]
            stats.append(jnp.where(a % 2 == 1, pltpu.roll(tile, DIM - 2, 1), tile))
        top = jnp.maximum(jnp.maximum(stats[0], stats[1]), jnp.maximum(stats[2], stats[3]))
        weight = [jnp.exp2((t - top) * SCALE) for t in stats]
        total = sum(pltpu.roll(w, PAIR // SUB, 1) * t for w, t in zip(weight, stats))
        share = pltpu.roll(1.0 / jnp.where(lane < PAIR // SUB, 1.0, total), DIM - PAIR // SUB, 1)
        value = jnp.zeros((GROUP, DIM), jnp.float32)
        for a, w in zip(at, weight):
            w = w * share
            w = jnp.concatenate([jnp.broadcast_to(w[:, c:c + 1], (SUB, DIM)) for c in range(GROUP // SUB)], axis=0)
            value = value + w * o_in[a].astype(jnp.float32)
        return value

    def r_copy(d):
        lanes = pl.ds(pl.multiple_of(x * LANES, LANES), LANES)
        if d == 0:
            return pltpu.make_async_copy(fx.at[0], out_ref.at[:, lanes], r_recv.at[0])
        return remote(fx.at[d], out_ref.at[:, lanes], r_send.at[0], r_recv.at[d], x_dev[d])

    for d in (2, 1, 3, 0):
        for r in range(OWN):
            ff[d, pl.ds(r, GROUP, stride=OWN), :] = finish(lax.rem(x + d, NX) * OWN + r)
        for h in range(GROUP):
            fx[d, :, h * DIM:(h + 1) * DIM] = ff[d, h * OWN:(h + 1) * OWN, :].astype(jnp.bfloat16)
        r_copy(d).start()
    for d in (1, 2, 3):
        x_copy(d).wait_send()
    for side in (0, 1):
        for chunk in range(CHUNKS):
            kv_copy(side, chunk, reach(side, chunk)).wait_send()
    for copy in q_copies(1, PLANE - 1) + all_copies(3):
        copy.wait_send()
    r_copy(0).wait()
    for d in (1, 3, 2):
        r_copy(d).wait()


def shards(queries, kv_cache, node_len, paths):
    rows, width = queries.shape
    bf16, f32, i32 = jnp.bfloat16, jnp.float32, jnp.int32
    dma = pltpu.SemaphoreType.DMA
    anywhere = pl.BlockSpec(memory_space=pl.ANY)
    return pl.pallas_call(
        kernel,
        out_shape=jax.ShapeDtypeStruct((rows, width), bf16),
        in_specs=[anywhere] * 4,
        out_specs=anywhere,
        scratch_shapes=[
            pltpu.VMEM((NX, OWN, LANES), bf16),
            pltpu.VMEM((GROUP * ROWS, DIM), f32),
            pltpu.VMEM((ROWS, GROUP, DIM), bf16),
            pltpu.VMEM((PLANE, PAIRS, PAIR, DIM), bf16),
            pltpu.VMEM((NZ, HEAD + 2 * TOKENS, DIM), bf16),
            pltpu.VMEM((1, 1), i32),
            pltpu.VMEM((ROWS, DEPTH), i32),
            pltpu.VMEM((PLANE, SUB, DIM), i32),
            pltpu.SMEM((PLANE, SUB, DIM), i32),
            pltpu.VMEM((2 * PLANE * NZ, GROUP, DIM), bf16),
            pltpu.VMEM((2 * PLANE * NZ, GROUP, DIM), bf16),
            pltpu.VMEM((PLANE * NZ, SUB, DIM), f32),
            pltpu.VMEM((PLANE * NZ, SUB, DIM), f32),
            pltpu.VMEM((NX, GROUP * OWN, DIM), f32),
            pltpu.VMEM((NX, OWN, LANES), bf16),
            dma((1,)), dma((NX,)),
            dma((2, CHUNKS)), dma((CHUNKS, FAR)),
            dma((1,)), dma((1,)),
            dma((1,)), dma((1,)),
            dma((NZ // BATCH,)), dma((NZ // BATCH,)),
            dma((NZ // BATCH,)), dma((NZ // BATCH,)),
            dma((1,)), dma((NX,)),
            dma((6,)),
        ],
        compiler_params=pltpu.CompilerParams(
            collective_id=0, has_side_effects=True, vmem_limit_bytes=56356864),
        cost_estimate=pl.CostEstimate(flops=1 << 30, bytes_accessed=1 << 22, transcendentals=1 << 21),
    )(queries, kv_cache, node_len.reshape(1, 1), paths)


def solution(mesh):
    return jax.shard_map(
        shards,
        mesh=mesh,
        in_specs=(
            P(("node", "head"), None),
            P(None, "node", None, "head"),
            P("node"),
            P("node", None),
        ),
        out_specs=P(("node", "head"), None),
        check_vma=False,
    )
```

```python
import math

import jax
import jax.numpy as jnp
from jax import lax
from jax.experimental import pallas as pl
from jax.experimental.pallas import tpu as pltpu
from jax.sharding import PartitionSpec as P

MESH = pl.DeviceIdType.MESH
NX, NY, NZ, NC = 4, 4, 16, 2
PLANE = NY * NC
FAR = NZ // 2
ROWS, GROUP, DIM, TOKENS, DEPTH = 32, 16, 128, 512, 4
PAIRS = ROWS // 2
PAIR = 2 * GROUP
OWN = ROWS // NX
LANES = GROUP * DIM
SUB = 8
EMPTY = -1e30
SCALE = math.log2(math.e) / math.sqrt(DIM)
CHUNKS = 4
CHUNK = 2 * TOKENS // CHUNKS
HEAD = 16
WARM = 3
BATCH = 4
SPAN = PLANE * BATCH


def ring_slot(side, hop):
    return hop if side == 0 else lax.rem(NZ - hop, NZ)


def reach(side, chunk):
    return FAR if side == chunk % 2 else FAR - 1


def chunk_rows(chunk):
    if isinstance(chunk, int) and chunk == 0:
        return pl.ds(0, HEAD + CHUNK)
    return pl.ds(pl.multiple_of(HEAD + chunk * CHUNK, 16), CHUNK)


def kernel(
    q_ref, kv_ref, len_s, paths_s, out_ref,
    qx, qf, qn, qplane, kvz, metav, metas, o_out, o_in, s_out, s_in, ff, fx,
    x_send, x_recv, kv_send, kv_recv, q_send, q_recv, m_send, m_recv,
    o_send, o_recv, s_send, s_recv, r_send, r_recv, own_sem,
):
    node = lax.axis_index("node")
    x = lax.axis_index("head")
    core = lax.rem(node, NC)
    z = lax.rem(node // NC, NZ)
    y = node // (NC * NZ)

    def dev(yy, zz, cc, xx):
        return ((yy * NZ + zz) * NC + cc, xx)

    z_dev = (dev(y, lax.rem(z + 1, NZ), core, x), dev(y, lax.rem(z + NZ - 1, NZ), core, x))
    x_dev = [None] + [dev(y, z, core, lax.rem(x + d, NX)) for d in range(1, NX)]
    p_dev = [dev(lax.rem(y + j // NC, NY), z, lax.rem(core + j % NC, NC), x) for j in range(PLANE)]
    b_dev = [dev(lax.rem(y + NY - j // NC, NY), z, lax.rem(core + j % NC, NC), x) for j in range(PLANE)]

    barrier = pltpu.get_barrier_semaphore()
    partners = list(z_dev) + x_dev[1:] + p_dev[1:]
    for partner in partners:
        pl.semaphore_signal(barrier, inc=1, device_id=partner, device_id_type=MESH)

    kv_own = [pltpu.make_async_copy(kv_ref.at[part, 0], kvz.at[0, pl.ds(HEAD + part * TOKENS, TOKENS)],
                                    own_sem.at[part]) for part in (0, 1)]
    for copy in kv_own:
        copy.start()
    length = jnp.full((HEAD, DIM), len_s[0], jnp.int32)
    upper = lax.broadcasted_iota(jnp.int32, (HEAD, DIM), 0) < HEAD // 2
    kvz[0, 0:HEAD, :] = jnp.where(upper, length >> 8, length & 255).astype(jnp.float32).astype(jnp.bfloat16)
    for copy in kv_own:
        copy.wait()
    pl.semaphore_wait(barrier, len(partners))

    def remote(src, dst, send, recv, to):
        return pltpu.make_async_remote_copy(
            src_ref=src, dst_ref=dst, send_sem=send, recv_sem=recv, device_id=to, device_id_type=MESH)

    def kv_copy(side, chunk, hop):
        rows = chunk_rows(chunk)
        return remote(kvz.at[ring_slot(side, hop - 1), rows], kvz.at[ring_slot(side, hop), rows],
                      kv_send.at[side, chunk], kv_recv.at[side, chunk, hop - 1], z_dev[side])

    def x_copy(d):
        lanes = pl.ds(pl.multiple_of(lax.rem(x + d, NX) * LANES, LANES), LANES)
        if d == 0:
            return pltpu.make_async_copy(q_ref.at[:, lanes], qx.at[x], x_recv.at[0])
        return remote(q_ref.at[:, lanes], qx.at[x], x_send.at[0], x_recv.at[d], x_dev[d])

    for side in (0, 1):
        kv_copy(side, 0, 1).start()
    for d in (2, 1, 3, 0):
        x_copy(d).start()
    for chunk in range(1, CHUNKS):
        for side in (0, 1):
            kv_copy(side, chunk, 1).start()

    def relay(hop, chunk, far=False):
        for side in (0, 1):
            last = reach(side, chunk) if far else FAR
            if not far or hop <= last:
                kv_copy(side, chunk, hop).wait_recv()
            if not far or hop < last:
                kv_copy(side, chunk, hop).wait_send()
                kv_copy(side, chunk, hop + 1).start()

    row = lax.broadcasted_iota(jnp.int32, (ROWS, DIM), 0)
    col = lax.broadcasted_iota(jnp.int32, (ROWS, DIM), 1)

    def upright(line):
        return jnp.sum(jnp.where(row == col, line, 0), axis=1, keepdims=True)

    spread = jnp.zeros((ROWS, DIM), jnp.int32)
    for r in range(ROWS):
        for j in range(DEPTH):
            spread = jnp.where((row == r) & (col == j), paths_s[j, r], spread)
    level = [spread[:, j:j + 1] for j in range(DEPTH)]
    key = level[0] * ROWS + row[:, 0:1]
    key_line = jnp.sum(jnp.where(row == col, key, 0), axis=0, keepdims=True)
    place_line = jnp.sum(jnp.where(key < key_line, 1, 0), axis=0, keepdims=True)
    place = upright(place_line)
    order_line = jnp.sum(jnp.where(place == col, row, 0), axis=0, keepdims=True)
    pair = jnp.zeros((ROWS, DIM), jnp.int32)
    for j in range(DEPTH):
        pair = jnp.maximum(pair, jnp.where(level[j] == col, place >> 1, 0))
    metav[0, 0:1, :] = jnp.max(pair, axis=0, keepdims=True)
    for j in range(DEPTH):
        n = jnp.sum(jnp.where(row == col, level[j], 0), axis=0, keepdims=True)
        partner = (((n >> 5) - y + NY) & (NY - 1)) * NC + (((n & 1) + core) & 1)
        hop = (z - ((n >> 1) & (NZ - 1)) + NZ) & (NZ - 1)
        t = jnp.where(hop == 0, 0, jnp.where(hop <= FAR, 2 * hop - 1, 2 * (NZ - hop)))
        at = (t >> 2) * SPAN + partner * BATCH + (t & 3)
        metav[0, 1 + j:2 + j, :] = at * 2 + (place_line & 1)
    metav[0, 5:6, :] = order_line
    metav[0, 6:8, :] = jnp.zeros((2, DIM), jnp.int32)
    own_meta = pltpu.make_async_copy(metav.at[0], metas.at[0], own_sem.at[4])
    own_meta.start()

    relay(1, 0)
    x_copy(0).wait()
    for d in (1, 3, 2):
        x_copy(d).wait_recv()
    for h in range(GROUP):
        for i in range(NX):
            qf[h * ROWS + i * OWN:h * ROWS + (i + 1) * OWN, :] = (
                qx[i, :, h * DIM:(h + 1) * DIM].astype(jnp.float32))
    relay(1, 1)
    for r in range(ROWS):
        qn[r] = qf[pl.ds(r, GROUP, stride=ROWS), :].astype(jnp.bfloat16)
    own_meta.wait()
    for p in range(ROWS):
        qplane[0, p // 2, (p % 2) * GROUP:(p % 2 + 1) * GROUP, :] = qn[metas[0, 5, p]]

    def q_copies(j, count=1):
        src = pl.ds(0, count)
        return (
            remote(qplane.at[src], qplane.at[pl.ds(j, count)], q_send.at[0], q_recv.at[0], p_dev[j]),
            remote(metav.at[src], metav.at[pl.ds(j, count)], m_send.at[0], m_recv.at[0], p_dev[j]),
        )

    for j in (4, 5, 2, 3, 6, 7, 1):
        for copy in q_copies(j):
            copy.start()

    lane = lax.broadcasted_iota(jnp.int32, (SUB, DIM), 1)
    token = lax.broadcasted_iota(jnp.int32, (1, TOKENS), 1).astype(jnp.float32)

    def ring_of(t):
        odd = lax.rem(t, 2)
        return odd * ((t + 1) // 2) + (1 - odd) * lax.rem(NZ - t // 2, NZ)

    def scores(t, j0):
        i = ring_of(t)
        n = (y * NZ + lax.rem(z + NZ - i, NZ)) * NC + core
        head = kvz[i, 0:HEAD, :].astype(jnp.float32)
        length = head[0:1, :] * 256.0 + head[HEAD // 2:HEAD // 2 + 1, :]
        bias = jnp.where(token < jnp.concatenate([length] * (TOKENS // DIM), axis=1), 0.0, EMPTY)
        lhs = jnp.concatenate([qplane[j, metas[j, 0, n]] for j in range(j0, j0 + 4)], axis=0)
        score = lax.dot_general(lhs, kvz[i, pl.ds(HEAD, TOKENS), :], (((1,), (1,)), ((), ())),
                                preferred_element_type=jnp.float32) + bias
        peak = jnp.max(score, axis=1, keepdims=True)
        prob = jnp.exp2((score - peak) * SCALE)
        return prob.astype(jnp.bfloat16), peak, jnp.sum(prob, axis=1, keepdims=True)

    def values(t, j0, prob, peak, total):
        i = ring_of(t)
        value = jnp.dot(prob, kvz[i, pl.ds(HEAD + TOKENS, TOKENS), :],
                        preferred_element_type=jnp.float32).astype(jnp.bfloat16)
        for j in range(j0, j0 + 4):
            base = (j - j0) * PAIR
            at = t // BATCH * SPAN + j * BATCH + lax.rem(t, BATCH)
            stat = jnp.zeros((SUB, DIM), jnp.float32)
            for c in range(PAIR // SUB):
                rows = slice(base + c * SUB, base + (c + 1) * SUB)
                stat = jnp.where(lane == c, peak[rows], stat)
                stat = jnp.where(lane == c + PAIR // SUB, total[rows], stat)
            for c in range(2):
                (o_in if j == 0 else o_out)[2 * at + c] = value[base + c * GROUP:base + (c + 1) * GROUP]
            (s_in if j == 0 else s_out)[at] = stat

    def attend(t):
        for j0 in (0, 4):
            values(t, j0, *scores(t, j0))

    def back_copies(j, b, first, count):
        at = pl.ds(b * SPAN + j * BATCH + first, count)
        both = pl.ds(2 * (b * SPAN + j * BATCH + first), 2 * count)
        return (
            remote(o_out.at[both], o_in.at[both], o_send.at[b], o_recv.at[b], b_dev[j]),
            remote(s_out.at[at], s_in.at[at], s_send.at[b], s_recv.at[b], b_dev[j]),
        )

    def send(b, first, count, partners=range(1, PLANE)):
        for j in partners:
            for copy in back_copies(j, b, first, count):
                copy.start()

    def all_copies(b):
        return back_copies(1, b, 0, SPAN - BATCH)

    for chunk in range(2, CHUNKS):
        relay(1, chunk)
    for hop in range(2, WARM + 1):
        for chunk in range(CHUNKS):
            relay(hop, chunk)
    relay(WARM + 1, 0)
    for copy in q_copies(1, PLANE - 1):
        copy.wait_recv()
    all_meta = pltpu.make_async_copy(metav.at[pl.ds(1, PLANE - 1)], metas.at[pl.ds(1, PLANE - 1)], own_sem.at[5])
    all_meta.start()
    all_meta.wait()

    def one_hop(b, carry):
        hop = WARM + 1 + b

        def one_chunk(q, carry):
            @pl.when((q >= 1) & (q < CHUNKS))
            def _():
                relay(hop, q)

            attend(BATCH * b + q)
            return carry

        lax.fori_loop(0, CHUNKS, one_chunk, 0)

        @pl.when(b < 2)
        def _():
            relay(hop + 1, 0)

        send(b, 0, BATCH)

        return carry

    lax.fori_loop(0, 3, one_hop, 0)
    relay(FAR - 1, 0, True)
    attend(12)
    relay(FAR - 1, 1, True)
    found = [(t, j0, scores(t, j0)) for t in (13, 14) for j0 in (0, 4)]
    relay(FAR - 1, 2, True)
    relay(FAR - 1, 3, True)
    for t, j0, parts in found:
        values(t, j0, *parts)
    send(3, 0, 3)
    relay(FAR, 0, True)
    relay(FAR, 1, True)
    found = [(j0, scores(15, j0)) for j0 in (4, 0)]
    relay(FAR, 2, True)
    relay(FAR, 3, True)
    for j0, parts in found:
        values(15, j0, *parts)
        send(3, 3, 1, range(max(j0, 1), j0 + 4))
    for b in range(3):
        for copy in all_copies(b):
            copy.wait()
    for copy in all_copies(3):
        copy.wait_recv()

    def finish(r):
        at = [metas[0, 1 + j, r] for j in range(DEPTH)]
        stats = []
        for a in at:
            tile = s_in[a // 2]
            stats.append(jnp.where(a % 2 == 1, pltpu.roll(tile, DIM - 2, 1), tile))
        top = jnp.maximum(jnp.maximum(stats[0], stats[1]), jnp.maximum(stats[2], stats[3]))
        weight = [jnp.exp2((t - top) * SCALE) for t in stats]
        total = sum(pltpu.roll(w, PAIR // SUB, 1) * t for w, t in zip(weight, stats))
        share = pltpu.roll(1.0 / jnp.where(lane < PAIR // SUB, 1.0, total), DIM - PAIR // SUB, 1)
        value = jnp.zeros((GROUP, DIM), jnp.float32)
        for a, w in zip(at, weight):
            w = w * share
            w = jnp.concatenate([jnp.broadcast_to(w[:, c:c + 1], (SUB, DIM)) for c in range(GROUP // SUB)], axis=0)
            value = value + w * o_in[a].astype(jnp.float32)
        return value

    def r_copy(d):
        lanes = pl.ds(pl.multiple_of(x * LANES, LANES), LANES)
        if d == 0:
            return pltpu.make_async_copy(fx.at[0], out_ref.at[:, lanes], r_recv.at[0])
        return remote(fx.at[d], out_ref.at[:, lanes], r_send.at[0], r_recv.at[d], x_dev[d])

    for d in (2, 1, 3, 0):
        for r in range(OWN):
            ff[d, pl.ds(r, GROUP, stride=OWN), :] = finish(lax.rem(x + d, NX) * OWN + r)
        for h in range(GROUP):
            fx[d, :, h * DIM:(h + 1) * DIM] = ff[d, h * OWN:(h + 1) * OWN, :].astype(jnp.bfloat16)
        r_copy(d).start()
    for d in (1, 2, 3):
        x_copy(d).wait_send()
    for side in (0, 1):
        for chunk in range(CHUNKS):
            kv_copy(side, chunk, reach(side, chunk)).wait_send()
    for copy in q_copies(1, PLANE - 1) + all_copies(3):
        copy.wait_send()
    r_copy(0).wait()
    for d in (1, 3, 2):
        r_copy(d).wait()


def shards(queries, kv_cache, node_len, paths):
    rows, width = queries.shape
    bf16, f32, i32 = jnp.bfloat16, jnp.float32, jnp.int32
    dma = pltpu.SemaphoreType.DMA
    anywhere = pl.BlockSpec(memory_space=pl.ANY)
    return pl.pallas_call(
        kernel,
        out_shape=jax.ShapeDtypeStruct((rows, width), bf16),
        in_specs=[anywhere] * 2 + [pl.BlockSpec(memory_space=pltpu.SMEM)] * 2,
        out_specs=anywhere,
        scratch_shapes=[
            pltpu.VMEM((NX, OWN, LANES), bf16),
            pltpu.VMEM((GROUP * ROWS, DIM), f32),
            pltpu.VMEM((ROWS, GROUP, DIM), bf16),
            pltpu.VMEM((PLANE, PAIRS, PAIR, DIM), bf16),
            pltpu.VMEM((NZ, HEAD + 2 * TOKENS, DIM), bf16),
            pltpu.VMEM((PLANE, SUB, DIM), i32),
            pltpu.SMEM((PLANE, SUB, DIM), i32),
            pltpu.VMEM((2 * PLANE * NZ, GROUP, DIM), bf16),
            pltpu.VMEM((2 * PLANE * NZ, GROUP, DIM), bf16),
            pltpu.VMEM((PLANE * NZ, SUB, DIM), f32),
            pltpu.VMEM((PLANE * NZ, SUB, DIM), f32),
            pltpu.VMEM((NX, GROUP * OWN, DIM), f32),
            pltpu.VMEM((NX, OWN, LANES), bf16),
            dma((1,)), dma((NX,)),
            dma((2, CHUNKS)), dma((2, CHUNKS, FAR)),
            dma((1,)), dma((1,)),
            dma((1,)), dma((1,)),
            dma((NZ // BATCH,)), dma((NZ // BATCH,)),
            dma((NZ // BATCH,)), dma((NZ // BATCH,)),
            dma((1,)), dma((NX,)),
            dma((6,)),
        ],
        compiler_params=pltpu.CompilerParams(
            collective_id=0, has_side_effects=True, vmem_limit_bytes=56356864),
        cost_estimate=pl.CostEstimate(flops=1 << 30, bytes_accessed=1 << 22, transcendentals=1 << 21),
    )(queries, kv_cache, node_len, paths.T)


def solution(mesh):
    return jax.shard_map(
        shards,
        mesh=mesh,
        in_specs=(
            P(("node", "head"), None),
            P(None, "node", None, "head"),
            P("node"),
            P("node", None),
        ),
        out_specs=P(("node", "head"), None),
        check_vma=False,
    )
```
